512 devices in a mesh: rep: 2 (over core), tab: 32 (over z, y_hi), tp: 8 (over y_lo, x).
Axes of the slice: x: 4, y: 8 (y_hi: 4, y_lo: 2; y = y_hi * 2 + y_lo), z: 8, core: 2. Of those that a mesh axis runs over, the one named last changes fastest.
Arguments:
- emb_rows: bfloat16 [512, 800, 512], P(('rep', 'tp'), 'tab'), may hold values from -6 to 6
- width_steps: int32 [800], P('tab'), may hold values from 1 to 8
- proj_weight: bfloat16 [800, 512, 192], P('tab', None, ('rep', 'tp')), may hold values from -0.25 to 0.25
- fm_weight: bfloat16 [400, 800], P('tp'), may hold values from -0.21875 to 0.21875
- lcb_weight: bfloat16 [400, 800], P('tp'), may hold values from -0.21875 to 0.21875
- mix_weight: bfloat16 [800, 192], P('tp'), may hold values from -1.796875 to 1.796875
- fm_cot: bfloat16 [512, 400, 192], P(('rep', 'tp', 'tab')), may hold values from -6 to 6
- lcb_cot: bfloat16 [512, 400, 192], P(('rep', 'tp', 'tab')), may hold values from -6 to 6
Outputs:
- fm_out: bfloat16 [512, 400, 192], P(('rep', 'tp', 'tab'))
- lcb_out: bfloat16 [512, 400, 192], P(('rep', 'tp', 'tab'))
- grad_fm: float32 [400, 800], P('tp')
- grad_lcb: float32 [400, 800], P('tp')
The draws below stay inside these ranges and needn't reach their ends.
All inputs are finite; a program needn't handle non-finite values.
Results may differ from the reference program's by a relative error of at most 0.0069.
Values may be sent and summed in bfloat16 or wider, within the bound.
No kernel may reach another device: no remote copies, remote signals or barrier semaphores. Data moves between devices by JAX's collectives and lax.ppermute only.
A program may use at most 64 MiB of HBM per device.

```python
import jax
import jax.numpy as jnp
from jax import lax

F = 800
D = 192
WMAX = 512
NF = 400
B = 512


def place_ends(array, key, smallest, high):
    longest = array.shape.index(max(array.shape))
    spots = []
    for shift in (0, 1):
        where = [jax.random.randint(jax.random.fold_in(key, axis), (), 0, length) for axis, length in enumerate(array.shape)]
        where[longest] = (where[longest] + shift) % array.shape[longest]
        spots.append(tuple(where))
    return array.at[spots[0]].set(smallest).at[spots[1]].set(high)


def with_spikes(array, rng, source, target, parts, factor):
    def block_of(dim):
        return (jnp.arange(array.shape[dim]) // (array.shape[dim] // parts)).reshape((-1,) + (1,) * (array.ndim - 1 - dim))

    one_side = jax.random.permutation(rng, parts)[block_of(target)]
    far = (block_of(target) + parts // 2) % parts
    return jnp.where((block_of(source) == one_side) | (block_of(source) == far), factor * array, array)


def shard_levels(key, dims, cuts, least, top_value):
    factor_of, own = 1.0, jax.random.fold_in(key, 6)
    for position, blocks in cuts:
        steps = jnp.exp(jax.random.uniform(jax.random.fold_in(own, position), (blocks,), jnp.float32, least / len(cuts), top_value / len(cuts)))
        factor_of = factor_of * jnp.repeat(steps, dims[position] // blocks).reshape([-1 if axis == position else 1 for axis in range(len(dims))])
    return factor_of


def normal_values(key, extent, width, bound, shards=(), kind=jnp.bfloat16):
    entries = jax.random.normal(key, extent, jnp.float32) * width
    if len(shards) > 0:
        entries = shard_levels(key, extent, shards, -0.22, 0.18) * entries
    return jnp.clip(entries, min=-bound, max=bound).astype(kind)


def gaussian_with(key, shape, width, limit, pieces, heavy, kind=jnp.bfloat16):
    array = width * jax.random.normal(key, shape, jnp.float32)
    if pieces:
        array = array * shard_levels(key, shape, pieces, -0.22, 0.18)
    return jnp.clip(with_spikes(array, jax.random.fold_in(key, 3), *heavy), -limit, limit).astype(kind)


def setup_inputs(seed: int = 0) -> dict:
    key_list = jax.random.split(jax.random.key(seed), 9)
    emb_rows = normal_values(key_list[0], (B, F, WMAX), 1.0, 6.0, ((0, 16), (1, 32)))
    width_steps = place_ends(jax.random.randint(key_list[1], (F,), 1, 9), jax.random.fold_in(key_list[1], 1), 1, 8).astype(jnp.int32)
    proj_weight = normal_values(key_list[2], (F, WMAX, D), WMAX ** -0.5, 0.25, ((0, 32), (2, 16)))
    fm_weight = normal_values(key_list[3], (NF, F), F ** -0.5, 0.21875, ((0, 8),))
    lcb_weight = normal_values(key_list[4], (NF, F), F ** -0.5, 0.21875, ((0, 8),))
    mix_weight = normal_values(key_list[5], (F, D), 0.3, 1.796875, ((0, 8),))
    fm_cot = gaussian_with(key_list[6], (B, NF, D), 1.0, 6.0, ((0, 512),), (0, 1, 16, 2.0))
    lcb_cot = gaussian_with(key_list[7], (B, NF, D), 1.0, 6.0, ((0, 512),), (0, 1, 16, 2.0))
    return dict(emb_rows=emb_rows, width_steps=width_steps, proj_weight=proj_weight, fm_weight=fm_weight, lcb_weight=lcb_weight, mix_weight=mix_weight, fm_cot=fm_cot, lcb_cot=lcb_cot)


epsilon = 1e-06

def rms_norm(values):
    inv_rms = lax.rsqrt(lax.optimization_barrier(jnp.mean(values * values, axis=-1, keepdims=True)) + epsilon)
    return (values * inv_rms, inv_rms)

def rms_back(values, grad_in):
    normed, inv_rms = rms_norm(values)
    return inv_rms * (grad_in - normed * lax.optimization_barrier(jnp.mean(grad_in * normed, axis=-1, keepdims=True)))

def reference(emb_rows, width_steps, proj_weight, fm_weight, lcb_weight, mix_weight, fm_cot, lcb_cot):
    columns = lax.broadcasted_iota(jnp.int32, (F, WMAX), 1)
    keep_mask = (columns < WMAX // 8 * width_steps[:, None]).astype(proj_weight.dtype)
    masked = (proj_weight * keep_mask[:, :, None]).astype(jnp.float32)

    def one_sample(sample_rows):
        features = jnp.einsum('fw,fwd->fd', sample_rows.astype(jnp.float32), masked).astype(jnp.bfloat16)
        feat_wide = features.astype(jnp.float32)
        products = (jnp.dot(features, features.T, preferred_element_type=jnp.float32) / D).astype(jnp.bfloat16)
        mixed_rows = jnp.dot(products, mix_weight, preferred_element_type=jnp.float32).astype(jnp.bfloat16)
        fm_pre = jnp.dot(fm_weight, mixed_rows, preferred_element_type=jnp.float32) + feat_wide[:NF]
        lcb_pre = jnp.dot(lcb_weight, features, preferred_element_type=jnp.float32) + feat_wide[NF:]
        return (features, mixed_rows, fm_pre, lcb_pre)
    features, mixed_rows, fm_pre, lcb_pre = lax.map(one_sample, emb_rows)
    fm_out = rms_norm(fm_pre)[0].astype(jnp.bfloat16)
    lcb_out = rms_norm(lcb_pre)[0].astype(jnp.bfloat16)
    fm_back = rms_back(fm_pre, fm_cot.astype(jnp.float32)).astype(jnp.bfloat16)
    lcb_back = rms_back(lcb_pre, lcb_cot.astype(jnp.float32)).astype(jnp.bfloat16)
    grad_fm = jnp.einsum('bnk,bfk->nf', fm_back.astype(jnp.float32), mixed_rows.astype(jnp.float32))
    grad_lcb = jnp.einsum('bnd,bfd->nf', lcb_back.astype(jnp.float32), features.astype(jnp.float32))
    return (fm_out, lcb_out, grad_fm, grad_lcb)
```

```python
import functools

import jax
import jax.numpy as jnp
from jax import lax
from jax.experimental import pallas as pl
from jax.experimental.pallas import tpu as pltpu
from jax.sharding import Mesh
from jax.sharding import PartitionSpec as P

F32 = jnp.float32
BF16 = jnp.bfloat16
EPS = 1e-06
VMEM_LIMIT = 48 * 1024 * 1024
SWAP = [(0, 1), (1, 0)]
TAB = ("z", "yh")
TP = ("yl", "x")

VM = pl.BlockSpec(memory_space=pltpu.VMEM)
SM = pl.BlockSpec(memory_space=pltpu.SMEM)


def call(kernel, outs, ins, scratch=(), smem=0, flops=0, size=0):
    return pl.pallas_call(
        kernel,
        out_shape=outs,
        in_specs=[SM] * smem + [VM] * (len(ins) - smem),
        out_specs=jax.tree.map(lambda _: VM, outs),
        scratch_shapes=list(scratch),
        compiler_params=pltpu.CompilerParams(vmem_limit_bytes=VMEM_LIMIT),
        cost_estimate=pl.CostEstimate(flops=flops, bytes_accessed=size, transcendentals=0),
    )(*ins)


def nt_dot(a, b):
    return lax.dot_general(a, b, (((1,), (1,)), ((), ())), preferred_element_type=F32)


def nn_dot(a, b):
    return lax.dot_general(a, b, (((1,), (0,)), ((), ())), preferred_element_type=F32)


def pack_kernel(fm_ref, lcb_ref, mix_ref, out_ref):
    out_ref[...] = jnp.zeros_like(out_ref)
    rows, cols = fm_ref.shape
    for k, ref in enumerate((fm_ref, lcb_ref)):
        for j in range(7):
            wide = min(128, cols - 128 * j)
            out_ref[k * 7 + j, :rows, :wide] = ref[:, 128 * j : 128 * j + wide]
    for j in range(4):
        out_ref[14 + j, :48, : mix_ref.shape[1]] = mix_ref[48 * j : 48 * j + 48, :]


def unpack_kernel(all_ref, fm_ref, lcb_ref, mix_ref, wide_ref, mixw_ref):
    for k, ref in enumerate((fm_ref, lcb_ref)):
        for i in range(8):
            for j in range(7):
                wide_ref[50 * i : 50 * i + 50, 128 * j : 128 * j + 128] = all_ref[i, 7 * k + j][:50].astype(F32)
        ref[...] = wide_ref[:, :800].astype(BF16)
    for i in range(8):
        for j in range(4):
            mixw_ref[48 * j : 48 * j + 48, 100 * i : 100 * i + 100] = all_ref[i, 14 + j][:48, :100].astype(F32)
    mix_ref[...] = mixw_ref[...].astype(BF16)


def project_kernel(idx_ref, emb_ref, emb_y_ref, *rest):
    w_refs, out_ref, acc_ref = rest[:-2], rest[-2], rest[-1]
    mine = idx_ref[0]
    tables, samples = emb_ref.shape[0], emb_ref.shape[1]
    for t in range(tables):
        weight = jnp.concatenate([ref[t] for ref in w_refs], axis=0)
        acc_ref[mine, pl.ds(t, samples, stride=32), :] = nt_dot(emb_ref[t], weight)
        acc_ref[1 - mine, pl.ds(t, samples, stride=32), :] = nt_dot(emb_y_ref[t], weight)
    for k in range(2):
        out_ref[k * samples : k * samples + samples] = acc_ref[k].reshape(samples, 32, 128).astype(BF16)


def rows_kernel(idx_ref, recv_ref, fm_ref, lcb_ref, mix_ref, fcot_ref, lcot_ref,
                fo_ref, lo_ref, keep_ref, send_ref, scr_ref, gt_ref, ft_ref, bf_ref, bl_ref):
    x, rep = idx_ref[1], idx_ref[2]
    for yl in range(2):
        for tab in range(32):
            scr_ref[yl, 25 * tab : 25 * tab + 25, :] = recv_ref[yl * 32 + tab][:25].astype(F32)
        gt_ref[yl] = scr_ref[yl].T
    for r in range(2):
        for yl in range(2):
            for place in range(4):
                far = lax.rem(place - x + 4, 4)
                start = pl.multiple_of((r + rep - 2 * r * rep) * 64 + far * 16, 16)
                row = r * 96 + yl * 48 + place * 12
                ft_ref[row : row + 12, :] = gt_ref[yl, pl.ds(start, 16), :][:12]
    feat = ft_ref[...]
    feat_b = feat.astype(BF16)
    inner = nt_dot(mix_ref[...], feat_b).astype(BF16)
    mixed_b = (nn_dot(inner, feat_b) * (1.0 / 192)).astype(BF16)

    def branch(rows, weight_ref, skip, cot_ref, out_ref, back_ref):
        pre = nt_dot(rows, weight_ref[...]) + skip
        inv = lax.rsqrt(jnp.sum(pre * pre, axis=0, keepdims=True) * (1.0 / 192) + EPS)
        normed = pre * inv
        out_ref[...] = normed.astype(BF16)
        cot = cot_ref[...].astype(F32)
        mean = jnp.sum(cot * normed, axis=0, keepdims=True) * (1.0 / 192)
        back = (inv * (cot - normed * mean)).T
        back_ref[...] = jnp.zeros_like(back_ref)
        for i in range(8):
            back_ref[56 * i : 56 * i + 50, :] = back[50 * i : 50 * i + 50]
        return back_ref[...].astype(BF16)

    back_l = branch(feat_b, lcb_ref, ft_ref[:, 400:800], lcot_ref, lo_ref, bl_ref)
    back_f = branch(mixed_b, fm_ref, ft_ref[:, :400], fcot_ref, fo_ref, bf_ref)
    first = jnp.full((1, 1), rep, jnp.int32) == 0
    keep = nn_dot(jnp.where(first, back_f, back_l), jnp.where(first, mixed_b, feat_b))
    send = nn_dot(jnp.where(first, back_l, back_f), jnp.where(first, feat_b, mixed_b))
    for i in range(8):
        keep_ref[i] = keep[56 * i : 56 * i + 56].astype(BF16)
        send_ref[i] = send[56 * i : 56 * i + 56].astype(BF16)


def per_device(emb_rows, width_steps, proj_weight, fm_weight, lcb_weight, mix_weight, fm_cot, lcb_cot):
    tables, widest = emb_rows.shape[1], emb_rows.shape[2]
    yl, x, rep = lax.axis_index("yl"), lax.axis_index("x"), lax.axis_index("rep")
    idx = jnp.stack([yl, x, rep]).astype(jnp.int32)

    emb = jnp.transpose(emb_rows, (1, 0, 2))
    emb_y = lax.ppermute(emb, "yl", SWAP)

    packed = call(
        pack_kernel,
        jax.ShapeDtypeStruct((18, 56, 128), BF16),
        [fm_weight, lcb_weight, mix_weight.T],
    )
    small = lax.all_gather(packed, TP)

    columns = lax.broadcasted_iota(jnp.int32, (tables, 1, widest), 2)
    keep_mask = columns < widest // 8 * width_steps[:, None, None]
    own = jnp.where(keep_mask, jnp.transpose(proj_weight, (0, 2, 1)), 0).astype(BF16)
    own = jnp.pad(own, ((0, 0), (0, 4), (0, 0)))
    up, down = [(i, (i + 1) % 4) for i in range(4)], [(i, (i + 3) % 4) for i in range(4)]
    half = (tables + 1) // 2
    before = lax.ppermute(own, "x", up)
    after = lax.ppermute(own, "x", down)
    far_a = lax.ppermute(before[:half], "x", up)
    far_b = lax.ppermute(after[half:], "x", down)
    far = jnp.concatenate([far_a, far_b], axis=0)
    mine = [own, after, far, before]
    other = [lax.ppermute(w, "rep", SWAP) for w in mine]

    chunks = call(
        project_kernel,
        jax.ShapeDtypeStruct((64, 32, 128), BF16),
        [idx, emb, emb_y] + mine + other,
        [pltpu.VMEM((2, 1024, 128), F32)],
        smem=1,
        flops=2 * 25 * 64 * 128 * 512,
        size=5 << 20,
    )
    recv = lax.all_to_all(chunks, ("yl",) + TAB, 0, 0, tiled=True)

    fm_full, lcb_full, mix_full = call(
        unpack_kernel,
        (
            jax.ShapeDtypeStruct((400, 800), BF16),
            jax.ShapeDtypeStruct((400, 800), BF16),
            jax.ShapeDtypeStruct((192, 800), BF16),
        ),
        [small],
        [pltpu.VMEM((400, 896), F32), pltpu.VMEM((192, 800), F32)],
        size=4 << 20,
    )
    branch_out = jax.ShapeDtypeStruct((192, 400), BF16)
    partial = jax.ShapeDtypeStruct((8, 56, 800), BF16)
    fm_out, lcb_out, keep, send = call(
        rows_kernel,
        (branch_out, branch_out, partial, partial),
        [idx, recv, fm_full, lcb_full, mix_full, fm_cot[0].T, lcb_cot[0].T],
        [
            pltpu.VMEM((2, 800, 128), F32),
            pltpu.VMEM((2, 128, 800), F32),
            pltpu.VMEM((192, 800), F32),
            pltpu.VMEM((448, 192), F32),
            pltpu.VMEM((448, 192), F32),
        ],
        smem=1,
        flops=700_000_000,
        size=5 << 20,
    )

    got = lax.ppermute(send, "rep", SWAP)
    pair = (keep.astype(F32) + got.astype(F32)).astype(BF16)
    shares = lax.all_to_all(pair, TP, 0, 0, tiled=True)
    share = jnp.sum(shares.astype(F32), axis=0).astype(BF16)
    share = jnp.pad(share, ((0, 8), (0, 224)))
    tiles = jnp.transpose(share.reshape(4, 16, 8, 128), (2, 0, 1, 3)).reshape(32, 16, 128)
    parts = lax.all_to_all(tiles, TAB, 0, 0, tiled=True)
    whole = jnp.sum(parts.astype(F32), axis=0).astype(BF16)
    spread = lax.all_to_all(jnp.broadcast_to(whole[None], (32, 16, 128)), TAB, 0, 0, tiled=True)
    swapped = lax.ppermute(spread, "rep", SWAP)

    def rows_of(blocks):
        wide = jnp.transpose(blocks.reshape(8, 4, 16, 128), (1, 2, 0, 3)).reshape(64, 1024)
        return wide[:50, :800].astype(F32)

    grad_a, grad_b = rows_of(spread), rows_of(swapped)
    first = rep == 0
    grad_fm = jnp.where(first, grad_a, grad_b)
    grad_lcb = jnp.where(first, grad_b, grad_a)
    return fm_out.T[None], lcb_out.T[None], grad_fm, grad_lcb


def solution(mesh):
    fine = Mesh(mesh.devices.reshape(2, 8, 4, 2, 4), ("rep", "z", "yh", "yl", "x"))
    samples = ("rep", "yl", "x") + TAB
    in_specs = (
        P(("rep", "yl", "x"), TAB, None),
        P(TAB),
        P(TAB, None, ("rep", "yl", "x")),
        P(TP, None),
        P(TP, None),
        P(TP, None),
        P(samples, None, None),
        P(samples, None, None),
    )
    out_specs = (P(samples, None, None), P(samples, None, None), P(TP, None), P(TP, None))
    return jax.shard_map(per_device, mesh=fine, in_specs=in_specs, out_specs=out_specs, check_vma=False)
```

```python
import functools

import jax
import jax.numpy as jnp
from jax import lax
from jax.experimental import pallas as pl
from jax.experimental.pallas import tpu as pltpu
from jax.sharding import Mesh
from jax.sharding import PartitionSpec as P

F32 = jnp.float32
BF16 = jnp.bfloat16
EPS = 1e-06
SOME = 16 * 1024 * 1024
SWAP = [(0, 1), (1, 0)]
TAB = ("z", "yh")
TP = ("yl", "x")

VM = pl.BlockSpec(memory_space=pltpu.VMEM)
SM = pl.BlockSpec(memory_space=pltpu.SMEM)


def call(kernel, outs, ins, scratch=(), smem=0, flops=0, size=0, specs=(), limit=None):
    return pl.pallas_call(
        kernel,
        out_shape=outs,
        in_specs=[SM] * smem + list(specs) + [VM] * (len(ins) - smem - len(specs)),
        out_specs=jax.tree.map(lambda _: VM, outs),
        scratch_shapes=list(scratch),
        compiler_params=pltpu.CompilerParams(vmem_limit_bytes=limit),
        cost_estimate=pl.CostEstimate(flops=flops, bytes_accessed=size, transcendentals=0),
    )(*ins)


def nt_dot(a, b):
    return lax.dot_general(a, b, (((1,), (1,)), ((), ())), preferred_element_type=F32)


def nn_dot(a, b):
    return lax.dot_general(a, b, (((1,), (0,)), ((), ())), preferred_element_type=F32)


def prep_kernel(idx_ref, steps_ref, proj_any, fm_any, lcb_any, mix_any, own_ref, pack_ref,
                proj_ref, fm_ref, lcb_ref, mix_ref, rows_ref, sems):
    copies = [
        pltpu.make_async_copy(src, dst, sems.at[k])
        for k, (src, dst) in enumerate(((proj_any, proj_ref), (fm_any, fm_ref), (lcb_any, lcb_ref), (mix_any, mix_ref)))
    ]
    for copy in copies:
        copy.start()
    tables, widest = proj_ref.shape[1], proj_ref.shape[2]
    columns = lax.broadcasted_iota(jnp.int32, (tables, widest), 1)
    keep = columns < widest // 8 * steps_ref[...]
    rows_ref[...] = jnp.zeros_like(rows_ref)
    pack_ref[...] = jnp.zeros_like(pack_ref)
    copies[0].wait()
    for j in range(12):
        masked = jnp.where(keep, proj_ref[j].astype(F32), 0.0)
        for c in range(4):
            rows_ref[c, pl.ds(j, tables, stride=16), :] = masked[:, 128 * c : 128 * c + 128]
    for t in range(tables):
        for c in range(4):
            own_ref[t, :, 128 * c : 128 * c + 128] = rows_ref[c, 16 * t : 16 * t + 16, :].astype(BF16)
    for copy in copies[1:]:
        copy.wait()
    rep = idx_ref[2]
    first = jnp.full((1, 1), rep, jnp.int32) == 0
    branch = jnp.where(first, fm_ref[...], lcb_ref[...])
    rows, cols = branch.shape
    for j in range(7):
        wide = min(128, cols - 128 * j)
        pack_ref[j, :rows, :wide] = branch[:, 128 * j : 128 * j + wide]
    for j in range(2):
        start = pl.multiple_of(rep * 96 + 48 * j, 16)
        pack_ref[7 + j, :48, : mix_ref.shape[1]] = mix_ref[pl.ds(start, 48), :]


def unpack_kernel(small_ref, branch_ref, mix_ref, wide_ref, mixw_ref):
    for k in range(2):
        for i in range(8):
            piece = small_ref.at[8 * k + i]
            for j in range(7):
                wide_ref[50 * i : 50 * i + 50, 128 * j : 128 * j + 128] = piece[j][:50].astype(F32)
            for j in range(2):
                row = 96 * k + 48 * j
                mixw_ref[row : row + 48, 100 * i : 100 * i + 100] = piece[7 + j][:48, :100].astype(F32)
        branch_ref[k] = wide_ref[:, :800].astype(BF16)
    mix_ref[...] = mixw_ref[...].astype(BF16)


def token_kernel(src_ref, out_ref):
    out_ref[...] = src_ref[0, :8, :128].astype(F32)


def project_kernel(idx_ref, token_ref, emb_ref, emb_a_ref, emb_b_ref, *rest):
    w_refs, out_ref, acc_ref = rest[:-2], rest[-2], rest[-1]
    tables, samples = emb_ref.shape[0], emb_ref.shape[1]
    free = lax.broadcasted_iota(jnp.int32, (samples, 128), 1) % 16 >= 12
    last = tables - 1
    extra = {}
    for t in [last] + list(range(last)):
        weight = jnp.concatenate([ref[t] for ref in w_refs], axis=0)
        cut = emb_a_ref.shape[0]
        for k, rows in enumerate((emb_ref[t], emb_a_ref[t] if t < cut else emb_b_ref[t - cut])):
            prod = nt_dot(rows, weight)
            if t == last:
                extra[k] = [jnp.where(free, pltpu.roll(prod, shift, 1), 0.0) for shift in (12, 8, 4)]
            else:
                if t < 3:
                    prod = prod + extra[k][t]
                slot = idx_ref[0] if k == 0 else 1 - idx_ref[0]
                acc_ref[slot, pl.ds(t, samples, stride=last), :] = prod
    for k in range(2):
        out_ref[k * samples : k * samples + samples] = acc_ref[k].reshape(samples, last, 128).astype(BF16)


def rows_kernel(idx_ref, recv_ref, weight_ref, mix_ref, fcot_ref, lcot_ref,
                fo_ref, lo_ref, keep_ref, send_ref, scr_ref, gt_ref, ft_ref, bf_ref, bl_ref):
    x, rep = idx_ref[1], idx_ref[2]
    place = lax.broadcasted_iota(jnp.int32, (32, 128), 1) % 16
    for yl in range(2):
        for tab in range(32):
            scr_ref[yl, 25 * tab : 25 * tab + 24, :] = recv_ref[yl * 32 + tab].astype(F32)
        last = [pltpu.roll(scr_ref[yl, pl.ds(k, 32, stride=25), :], 116 + 4 * k, 1) for k in range(3)]
        scr_ref[yl, pl.ds(24, 32, stride=25), :] = jnp.where(place < 4, last[0], jnp.where(place < 8, last[1], last[2]))
        gt_ref[yl] = scr_ref[yl].T
    for r in range(2):
        for yl in range(2):
            for spot in range(4):
                far = lax.rem(spot - x + 4, 4)
                start = pl.multiple_of((r + rep - 2 * r * rep) * 64 + far * 16, 16)
                row = r * 96 + yl * 48 + spot * 12
                ft_ref[row : row + 12, :] = gt_ref[yl, pl.ds(start, 16), :][:12]
    feat = ft_ref[...]
    feat_b = feat.astype(BF16)
    inner = nt_dot(mix_ref[...], feat_b)
    high = inner.astype(BF16)
    low = (inner - high.astype(F32)).astype(BF16)
    mixed_b = ((nn_dot(high, feat_b) + nn_dot(low, feat_b)) * (1.0 / 192)).astype(BF16)

    def branch(rows, weight, skip, cot_ref, out_ref, back_ref):
        pre = nt_dot(rows, weight) + skip
        inv = lax.rsqrt(jnp.sum(pre * pre, axis=0, keepdims=True) * (1.0 / 192) + EPS)
        normed = pre * inv
        out_ref[...] = normed.astype(BF16)
        cot = cot_ref[...].astype(F32)
        mean = jnp.sum(cot * normed, axis=0, keepdims=True) * (1.0 / 192)
        back = (inv * (cot - normed * mean)).T
        back_ref[...] = jnp.zeros_like(back_ref)
        for i in range(8):
            back_ref[56 * i : 56 * i + 50, :] = back[50 * i : 50 * i + 50]
        return back_ref[...].astype(BF16)

    back_l = branch(feat_b, weight_ref[1], ft_ref[:, 400:800], lcot_ref, lo_ref, bl_ref)
    back_f = branch(mixed_b, weight_ref[0], ft_ref[:, :400], fcot_ref, fo_ref, bf_ref)
    first = jnp.full((1, 1), rep, jnp.int32) == 0
    keep = nn_dot(jnp.where(first, back_f, back_l), jnp.where(first, mixed_b, feat_b))
    send = nn_dot(jnp.where(first, back_l, back_f), jnp.where(first, feat_b, mixed_b))
    for i in range(8):
        keep_ref[i] = keep[56 * i : 56 * i + 56].astype(BF16)
        send_ref[i] = send[56 * i : 56 * i + 56].astype(BF16)


def per_device(emb_rows, width_steps, proj_weight, fm_weight, lcb_weight, mix_weight, fm_cot, lcb_cot):
    tables, widest = emb_rows.shape[1], emb_rows.shape[2]
    yl, x, rep = lax.axis_index("yl"), lax.axis_index("x"), lax.axis_index("rep")
    idx = jnp.stack([yl, x, rep]).astype(jnp.int32)

    emb = jnp.transpose(emb_rows, (1, 0, 2))
    cut = (tables + 1) // 2
    emb_a = lax.ppermute(emb[:cut], "yl", SWAP)
    rest, emb_a = lax.optimization_barrier((emb[cut:], emb_a))
    emb_b = lax.ppermute(rest, "yl", SWAP)
    token = pl.pallas_call(
        token_kernel,
        out_shape=jax.ShapeDtypeStruct((8, 128), F32),
        grid=(1,),
        in_specs=[pl.BlockSpec((1, 32, 512), lambda i: (0, 0, 0))],
        out_specs=pl.BlockSpec((8, 128), lambda i: (0, 0)),
        cost_estimate=pl.CostEstimate(flops=20_000_000_000, bytes_accessed=1 << 14, transcendentals=0),
    )(emb_b)

    proj = jnp.transpose(proj_weight, (2, 0, 1))
    own, packed = pl.pallas_call(
        prep_kernel,
        out_shape=(
            jax.ShapeDtypeStruct((tables, 16, widest), BF16),
            jax.ShapeDtypeStruct((9, 56, 128), BF16),
        ),
        in_specs=[SM, VM] + [pl.BlockSpec(memory_space=pl.ANY)] * 4,
        out_specs=(VM, VM),
        scratch_shapes=[
            pltpu.VMEM(proj.shape, BF16),
            pltpu.VMEM(fm_weight.shape, BF16),
            pltpu.VMEM(lcb_weight.shape, BF16),
            pltpu.VMEM(mix_weight.shape[::-1], BF16),
            pltpu.VMEM((4, 16 * tables, 128), F32),
            pltpu.SemaphoreType.DMA((4,)),
        ],
        cost_estimate=pl.CostEstimate(flops=1 << 20, bytes_accessed=2 << 20, transcendentals=0),
    )(idx, width_steps[:, None], proj, fm_weight, lcb_weight, mix_weight.T)
    small = lax.all_gather(packed, ("rep",) + TP)

    up, down = [(i, (i + 1) % 4) for i in range(4)], [(i, (i + 3) % 4) for i in range(4)]
    half = (tables + 1) // 2
    before = lax.ppermute(own, "x", up)
    after = lax.ppermute(own, "x", down)
    own_o = lax.ppermute(own, "rep", SWAP)
    far_a = lax.ppermute(before[:half], "x", up)
    far_b = lax.ppermute(after[half:], "x", down)
    near_o = lax.ppermute(jnp.stack([before, after]), "rep", SWAP)
    far = jnp.concatenate([far_a, far_b], axis=0)
    far_o = lax.ppermute(far, "rep", SWAP)
    mine = [own, after, far, before]
    other = [own_o, near_o[1], far_o, near_o[0]]

    chunks = call(
        project_kernel,
        jax.ShapeDtypeStruct((64, 24, 128), BF16),
        [idx, token, emb, emb_a, emb_b] + mine + other,
        [pltpu.VMEM((2, 768, 128), F32)],
        smem=1,
        limit=SOME,
        specs=[pl.BlockSpec(memory_space=pl.ANY)],
        flops=2 * 25 * 64 * 128 * 512,
        size=5 << 20,
    )
    recv = lax.all_to_all(chunks, ("yl",) + TAB, 0, 0, tiled=True)

    weights, mix_full = call(
        unpack_kernel,
        (jax.ShapeDtypeStruct((2, 400, 800), BF16), jax.ShapeDtypeStruct((192, 800), BF16)),
        [small],
        [pltpu.VMEM((400, 896), F32), pltpu.VMEM((192, 800), F32)],
        size=4 << 20,
        limit=SOME,
    )
    branch_out = jax.ShapeDtypeStruct((192, 400), BF16)
    partial = jax.ShapeDtypeStruct((8, 56, 800), BF16)
    fm_out, lcb_out, keep, send = call(
        rows_kernel,
        (branch_out, branch_out, partial, partial),
        [idx, recv, weights, mix_full, fm_cot[0].T, lcb_cot[0].T],
        [
            pltpu.VMEM((2, 800, 128), F32),
            pltpu.VMEM((2, 128, 800), F32),
            pltpu.VMEM((192, 800), F32),
            pltpu.VMEM((448, 192), F32),
            pltpu.VMEM((448, 192), F32),
        ],
        smem=1,
        limit=SOME,
        flops=700_000_000,
        size=5 << 20,
    )

    got = lax.ppermute(send, "rep", SWAP)
    pair = (keep.astype(F32) + got.astype(F32)).astype(BF16)
    shares = lax.all_to_all(pair, TP, 0, 0, tiled=True)
    share = jnp.sum(shares.astype(F32), axis=0).astype(BF16)
    share = jnp.pad(share, ((0, 0), (0, 224)))
    tiles = jnp.transpose(share.reshape(56, 8, 128), (1, 0, 2))
    over_z = jnp.sum(lax.all_to_all(tiles, "z", 0, 0, tiled=True).astype(F32), axis=0)
    parts = lax.all_to_all(jnp.broadcast_to(over_z[None], (4, 56, 128)), "yh", 0, 0, tiled=True)
    whole = jnp.sum(parts, axis=0).astype(BF16)
    spread = lax.all_to_all(jnp.broadcast_to(whole[None], (8, 56, 128)), "z", 0, 0, tiled=True)
    swapped = lax.ppermute(spread, "rep", SWAP)

    def rows_of(blocks):
        return jnp.transpose(blocks, (1, 0, 2)).reshape(56, 1024)[:50, :800].astype(F32)

    grad_a, grad_b = rows_of(spread), rows_of(swapped)
    first = rep == 0
    grad_fm = jnp.where(first, grad_a, grad_b)
    grad_lcb = jnp.where(first, grad_b, grad_a)
    return fm_out.T[None], lcb_out.T[None], grad_fm, grad_lcb


def solution(mesh):
    fine = Mesh(mesh.devices.reshape(2, 8, 4, 2, 4), ("rep", "z", "yh", "yl", "x"))
    samples = ("rep", "yl", "x") + TAB
    in_specs = (
        P(("rep", "yl", "x"), TAB, None),
        P(TAB),
        P(TAB, None, ("rep", "yl", "x")),
        P(TP, None),
        P(TP, None),
        P(TP, None),
        P(samples, None, None),
        P(samples, None, None),
    )
    out_specs = (P(samples, None, None), P(samples, None, None), P(TP, None), P(TP, None))
    return jax.shard_map(per_device, mesh=fine, in_specs=in_specs, out_specs=out_specs, check_vma=False)
```

```python
import functools

import jax
import jax.numpy as jnp
from jax import lax
from jax.experimental import pallas as pl
from jax.experimental.pallas import tpu as pltpu
from jax.sharding import Mesh
from jax.sharding import PartitionSpec as P

F32 = jnp.float32
BF16 = jnp.bfloat16
EPS = 1e-06
SOME = 16 * 1024 * 1024
SWAP = [(0, 1), (1, 0)]
TAB = ("z", "yh")
TP = ("yl", "x")

VM = pl.BlockSpec(memory_space=pltpu.VMEM)
SM = pl.BlockSpec(memory_space=pltpu.SMEM)


def call(kernel, outs, ins, scratch=(), flops=0, size=0, limit=None):
    return pl.pallas_call(
        kernel,
        out_shape=outs,
        in_specs=[VM] * len(ins),
        out_specs=jax.tree.map(lambda _: VM, outs),
        scratch_shapes=list(scratch),
        compiler_params=pltpu.CompilerParams(vmem_limit_bytes=limit),
        cost_estimate=pl.CostEstimate(flops=flops, bytes_accessed=size, transcendentals=0),
    )(*ins)


def nt_dot(a, b):
    return lax.dot_general(a, b, (((1,), (1,)), ((), ())), preferred_element_type=F32)


def nn_dot(a, b):
    return lax.dot_general(a, b, (((1,), (0,)), ((), ())), preferred_element_type=F32)


def prep_kernel(steps_ref, proj_any, fm_any, lcb_any, mix_any, own_ref, pack_ref,
                proj_ref, fm_ref, lcb_ref, mix_ref, rows_ref, sems):
    copies = [
        pltpu.make_async_copy(src, dst, sems.at[k])
        for k, (src, dst) in enumerate(((proj_any, proj_ref), (fm_any, fm_ref), (lcb_any, lcb_ref), (mix_any, mix_ref)))
    ]
    for copy in copies:
        copy.start()
    tables, widest = proj_ref.shape[1], proj_ref.shape[2]
    columns = lax.broadcasted_iota(jnp.int32, (tables, widest), 1)
    table = lax.broadcasted_iota(jnp.int32, (tables, widest), 0)
    width = jnp.zeros((tables, widest), jnp.int32)
    for t in range(tables):
        width = jnp.where(table == t, steps_ref[t], width)
    keep = columns < widest // 8 * width
    rows_ref[...] = jnp.zeros_like(rows_ref)
    pack_ref[...] = jnp.zeros_like(pack_ref)
    copies[0].wait()
    for j in range(12):
        masked = jnp.where(keep, proj_ref[j].astype(F32), 0.0)
        for c in range(4):
            rows_ref[c, pl.ds(j, tables, stride=16), :] = masked[:, 128 * c : 128 * c + 128]
    for t in range(tables):
        for c in range(4):
            own_ref[t, :, 128 * c : 128 * c + 128] = rows_ref[c, 16 * t : 16 * t + 16, :].astype(BF16)
    for copy in copies[1:]:
        copy.wait()
    rep = lax.axis_index("rep")
    first = jnp.full((1, 1), rep, jnp.int32) == 0
    branch = jnp.where(first, fm_ref[...], lcb_ref[...])
    rows, cols = branch.shape
    for j in range(7):
        wide = min(128, cols - 128 * j)
        pack_ref[j, :rows, :wide] = branch[:, 128 * j : 128 * j + wide]
    for j in range(2):
        start = pl.multiple_of(rep * 96 + 48 * j, 16)
        pack_ref[7 + j, :48, : mix_ref.shape[1]] = mix_ref[pl.ds(start, 48), :]


def unpack_kernel(small_ref, branch_ref, mix_ref, wide_ref, mixw_ref):
    for k in range(2):
        for i in range(8):
            piece = small_ref.at[8 * k + i]
            for j in range(7):
                wide_ref[50 * i : 50 * i + 50, 128 * j : 128 * j + 128] = piece[j][:50].astype(F32)
            for j in range(2):
                row = 96 * k + 48 * j
                mixw_ref[row : row + 48, 100 * i : 100 * i + 100] = piece[7 + j][:48, :100].astype(F32)
        branch_ref[k] = wide_ref[:, :800].astype(BF16)
    mix_ref[...] = mixw_ref[...].astype(BF16)


def project_kernel(emb_ref, emb_y_ref, *rest):
    w_refs, out_ref, acc_ref = rest[:-2], rest[-2], rest[-1]
    mine = lax.axis_index("yl")
    far_cut = w_refs[2].shape[0]
    tables, samples = emb_ref.shape[0], emb_ref.shape[1]
    free = lax.broadcasted_iota(jnp.int32, (samples, 128), 1) % 16 >= 12
    last = tables - 1
    extra = {}
    for t in [last] + list(range(last)):
        far = w_refs[2][t] if t < far_cut else w_refs[3][t - far_cut]
        weight = jnp.concatenate([w_refs[0][t], w_refs[1][t], far] + [ref[t] for ref in w_refs[4:]], axis=0)
        for k, ref in enumerate((emb_ref, emb_y_ref)):
            prod = nt_dot(ref[t], weight)
            if t == last:
                extra[k] = [jnp.where(free, pltpu.roll(prod, shift, 1), 0.0) for shift in (12, 8, 4)]
            else:
                if t < 3:
                    prod = prod + extra[k][t]
                slot = mine if k == 0 else 1 - mine
                acc_ref[slot, pl.ds(t, samples, stride=last), :] = prod
    for k in range(2):
        out_ref[k * samples : k * samples + samples] = acc_ref[k].reshape(samples, last, 128).astype(BF16)


def rows_kernel(recv_ref, weight_ref, mix_ref, fcot_ref, lcot_ref,
                fo_ref, lo_ref, keep_ref, send_ref, scr_ref, gt_ref, ft_ref, bf_ref, bl_ref):
    x, rep = lax.axis_index("x"), lax.axis_index("rep")
    place = lax.broadcasted_iota(jnp.int32, (32, 128), 1) % 16
    for yl in range(2):
        for tab in range(32):
            scr_ref[yl, 25 * tab : 25 * tab + 24, :] = recv_ref[yl * 32 + tab].astype(F32)
        last = [pltpu.roll(scr_ref[yl, pl.ds(k, 32, stride=25), :], 116 + 4 * k, 1) for k in range(3)]
        scr_ref[yl, pl.ds(24, 32, stride=25), :] = jnp.where(place < 4, last[0], jnp.where(place < 8, last[1], last[2]))
        gt_ref[yl] = scr_ref[yl].T
    for r in range(2):
        for yl in range(2):
            for spot in range(4):
                far = jnp.bitwise_xor(x, spot)
                start = pl.multiple_of((r + rep - 2 * r * rep) * 64 + far * 16, 16)
                row = r * 96 + yl * 48 + spot * 12
                ft_ref[row : row + 12, :] = gt_ref[yl, pl.ds(start, 16), :][:12]
    feat = ft_ref[...]
    feat_b = feat.astype(BF16)
    inner = nt_dot(mix_ref[...], feat_b)
    high = inner.astype(BF16)
    low = (inner - high.astype(F32)).astype(BF16)
    mixed_b = ((nn_dot(high, feat_b) + nn_dot(low, feat_b)) * (1.0 / 192)).astype(BF16)

    def branch(rows, weight, skip, cot_ref, out_ref, back_ref):
        pre = nt_dot(rows, weight) + skip
        inv = lax.rsqrt(jnp.sum(pre * pre, axis=0, keepdims=True) * (1.0 / 192) + EPS)
        normed = pre * inv
        out_ref[...] = normed.astype(BF16)
        cot = cot_ref[...].astype(F32)
        mean = jnp.sum(cot * normed, axis=0, keepdims=True) * (1.0 / 192)
        back = (inv * (cot - normed * mean)).T
        back_ref[...] = jnp.zeros_like(back_ref)
        for i in range(8):
            back_ref[56 * i : 56 * i + 50, :] = back[50 * i : 50 * i + 50]
        return back_ref[...].astype(BF16)

    back_l = branch(feat_b, weight_ref[1], ft_ref[:, 400:800], lcot_ref, lo_ref, bl_ref)
    back_f = branch(mixed_b, weight_ref[0], ft_ref[:, :400], fcot_ref, fo_ref, bf_ref)
    first = jnp.full((1, 1), rep, jnp.int32) == 0
    keep = nn_dot(jnp.where(first, back_f, back_l), jnp.where(first, mixed_b, feat_b))
    send = nn_dot(jnp.where(first, back_l, back_f), jnp.where(first, feat_b, mixed_b))
    for i in range(8):
        keep_ref[i] = keep[56 * i : 56 * i + 56].astype(BF16)
        send_ref[i] = send[56 * i : 56 * i + 56].astype(BF16)


def per_device(emb_rows, width_steps, proj_weight, fm_weight, lcb_weight, mix_weight, fm_cot, lcb_cot):
    tables, widest = emb_rows.shape[1], emb_rows.shape[2]
    emb = jnp.transpose(emb_rows, (1, 0, 2))
    emb_y = lax.ppermute(emb, "yl", SWAP)

    proj = jnp.transpose(proj_weight, (2, 0, 1))
    own, packed = pl.pallas_call(
        prep_kernel,
        out_shape=(
            jax.ShapeDtypeStruct((tables, 16, widest), BF16),
            jax.ShapeDtypeStruct((9, 56, 128), BF16),
        ),
        in_specs=[SM] + [pl.BlockSpec(memory_space=pl.ANY)] * 4,
        out_specs=(VM, VM),
        scratch_shapes=[
            pltpu.VMEM(proj.shape, BF16),
            pltpu.VMEM(fm_weight.shape, BF16),
            pltpu.VMEM(lcb_weight.shape, BF16),
            pltpu.VMEM(mix_weight.shape[::-1], BF16),
            pltpu.VMEM((4, 16 * tables, 128), F32),
            pltpu.SemaphoreType.DMA((4,)),
        ],
        cost_estimate=pl.CostEstimate(flops=1 << 20, bytes_accessed=2 << 20, transcendentals=0),
    )(width_steps, proj, fm_weight, lcb_weight, mix_weight.T)
    small = lax.all_gather(packed, ("rep",) + TP)

    side, back = [(i, i ^ 1) for i in range(4)], [(i, i ^ 3) for i in range(4)]
    half = (tables + 1) // 2
    near = lax.ppermute(own, "x", side)
    next_ = lax.ppermute(own, "x", back)
    far_a = lax.ppermute(near[:half], "x", back)
    far_b = lax.ppermute(next_[half:], "x", side)
    far = jnp.concatenate([far_a, far_b], axis=0)
    mine = [own, near, far_a, far_b, next_]
    other = [lax.ppermute(w, "rep", SWAP) for w in (own, near, far, next_)]

    chunks = call(
        project_kernel,
        jax.ShapeDtypeStruct((64, 24, 128), BF16),
        [emb, emb_y] + mine + other,
        [pltpu.VMEM((2, 768, 128), F32)],
        limit=SOME,
        flops=2 * 25 * 64 * 128 * 512,
        size=5 << 20,
    )
    recv = lax.all_to_all(chunks, ("yl",) + TAB, 0, 0, tiled=True)
    recv, small = lax.optimization_barrier((recv, small))

    weights, mix_full = call(
        unpack_kernel,
        (jax.ShapeDtypeStruct((2, 400, 800), BF16), jax.ShapeDtypeStruct((192, 800), BF16)),
        [small],
        [pltpu.VMEM((400, 896), F32), pltpu.VMEM((192, 800), F32)],
        size=4 << 20,
        limit=SOME,
    )
    branch_out = jax.ShapeDtypeStruct((192, 400), BF16)
    partial = jax.ShapeDtypeStruct((8, 56, 800), BF16)
    fm_out, lcb_out, keep, send = call(
        rows_kernel,
        (branch_out, branch_out, partial, partial),
        [recv, weights, mix_full, fm_cot[0].T, lcb_cot[0].T],
        [
            pltpu.VMEM((2, 800, 128), F32),
            pltpu.VMEM((2, 128, 800), F32),
            pltpu.VMEM((192, 800), F32),
            pltpu.VMEM((448, 192), F32),
            pltpu.VMEM((448, 192), F32),
        ],
        limit=SOME,
        flops=700_000_000,
        size=5 << 20,
    )

    got = lax.ppermute(send, "rep", SWAP)
    pair = (keep.astype(F32) + got.astype(F32)).astype(BF16)
    shares = lax.all_to_all(pair, TP, 0, 0, tiled=True)
    share = jnp.sum(shares.astype(F32), axis=0).astype(BF16)
    share = jnp.pad(share, ((0, 8), (0, 224)))
    tiles = jnp.transpose(share.reshape(4, 16, 8, 128), (2, 0, 1, 3)).reshape(32, 16, 128)
    parts = lax.all_to_all(tiles, TAB, 0, 0, tiled=True)
    whole = jnp.sum(parts.astype(F32), axis=0).astype(BF16)
    spread = lax.all_to_all(jnp.broadcast_to(whole[None], (32, 16, 128)), TAB, 0, 0, tiled=True)
    swapped = lax.ppermute(spread, "rep", SWAP)

    def rows_of(blocks):
        wide = jnp.transpose(blocks.reshape(8, 4, 16, 128), (1, 2, 0, 3)).reshape(64, 1024)
        return wide[:50, :800].astype(F32)

    grad_a, grad_b = rows_of(spread), rows_of(swapped)
    first = lax.axis_index("rep") == 0
    grad_fm = jnp.where(first, grad_a, grad_b)
    grad_lcb = jnp.where(first, grad_b, grad_a)
    return fm_out.T[None], lcb_out.T[None], grad_fm, grad_lcb


def solution(mesh):
    fine = Mesh(mesh.devices.reshape(2, 8, 4, 2, 4), ("rep", "z", "yh", "yl", "x"))
    samples = ("rep", "yl", "x") + TAB
    in_specs = (
        P(("rep", "yl", "x"), TAB, None),
        P(TAB),
        P(TAB, None, ("rep", "yl", "x")),
        P(TP, None),
        P(TP, None),
        P(TP, None),
        P(samples, None, None),
        P(samples, None, None),
    )
    out_specs = (P(samples, None, None), P(samples, None, None), P(TP, None), P(TP, None))
    return jax.shard_map(per_device, mesh=fine, in_specs=in_specs, out_specs=out_specs, check_vma=False)
```

```python
import functools

import jax
import jax.numpy as jnp
from jax import lax
from jax.experimental import pallas as pl
from jax.experimental.pallas import tpu as pltpu
from jax.sharding import Mesh
from jax.sharding import PartitionSpec as P

F32 = jnp.float32
BF16 = jnp.bfloat16
EPS = 1e-06
SOME = 16 * 1024 * 1024
SWAP = [(0, 1), (1, 0)]
TAB = ("z", "yh")
TP = ("yl", "x")
GROUPS = [
    [(((rep * 4 + (yh - yl) % 4) * 2 + yl) * 4) + x for rep in range(2) for yl in range(2) for x in range(4)]
    for yh in range(4)
]

VM = pl.BlockSpec(memory_space=pltpu.VMEM)
SM = pl.BlockSpec(memory_space=pltpu.SMEM)


def call(kernel, outs, ins, scratch=(), flops=0, size=0, limit=None):
    return pl.pallas_call(
        kernel,
        out_shape=outs,
        in_specs=[VM] * len(ins),
        out_specs=jax.tree.map(lambda _: VM, outs),
        scratch_shapes=list(scratch),
        compiler_params=pltpu.CompilerParams(vmem_limit_bytes=limit),
        cost_estimate=pl.CostEstimate(flops=flops, bytes_accessed=size, transcendentals=0),
    )(*ins)


def nt_dot(a, b):
    return lax.dot_general(a, b, (((1,), (1,)), ((), ())), preferred_element_type=F32)


def nn_dot(a, b):
    return lax.dot_general(a, b, (((1,), (0,)), ((), ())), preferred_element_type=F32)


def prep_kernel(steps_ref, proj_any, fm_any, lcb_any, mix_any, own_ref, pack_ref,
                proj_ref, fm_ref, lcb_ref, mix_ref, rows_ref, sems):
    copies = [
        pltpu.make_async_copy(src, dst, sems.at[k])
        for k, (src, dst) in enumerate(((proj_any, proj_ref), (fm_any, fm_ref), (lcb_any, lcb_ref), (mix_any, mix_ref)))
    ]
    for copy in copies:
        copy.start()
    tables, widest = proj_ref.shape[1], proj_ref.shape[2]
    columns = lax.broadcasted_iota(jnp.int32, (tables, widest), 1)
    table = lax.broadcasted_iota(jnp.int32, (tables, widest), 0)
    width = jnp.zeros((tables, widest), jnp.int32)
    for t in range(tables):
        width = jnp.where(table == t, steps_ref[t], width)
    keep = columns < widest // 8 * width
    rows_ref[...] = jnp.zeros_like(rows_ref)
    pack_ref[...] = jnp.zeros_like(pack_ref)
    copies[0].wait()
    for j in range(12):
        masked = jnp.where(keep, proj_ref[j].astype(F32), 0.0)
        for c in range(4):
            rows_ref[c, pl.ds(j, tables, stride=16), :] = masked[:, 128 * c : 128 * c + 128]
    for t in range(tables):
        for c in range(4):
            own_ref[t, :, 128 * c : 128 * c + 128] = rows_ref[c, 16 * t : 16 * t + 16, :].astype(BF16)
    for copy in copies[1:]:
        copy.wait()
    rep = lax.axis_index("rep")
    first = jnp.full((1, 1), rep, jnp.int32) == 0
    branch = jnp.where(first, fm_ref[...], lcb_ref[...])
    rows, cols = branch.shape
    for j in range(7):
        wide = min(128, cols - 128 * j)
        pack_ref[j, :rows, :wide] = branch[:, 128 * j : 128 * j + wide]
    for j in range(2):
        start = pl.multiple_of(rep * 96 + 48 * j, 16)
        pack_ref[7 + j, :48, : mix_ref.shape[1]] = mix_ref[pl.ds(start, 48), :]


def unpack_kernel(small_ref, branch_ref, mix_ref, wide_ref, mixw_ref):
    for k in range(2):
        for i in range(8):
            piece = small_ref.at[8 * k + i]
            for j in range(7):
                wide_ref[50 * i : 50 * i + 50, 128 * j : 128 * j + 128] = piece[j][:50].astype(F32)
            for j in range(2):
                row = 96 * k + 48 * j
                mixw_ref[row : row + 48, 100 * i : 100 * i + 100] = piece[7 + j][:48, :100].astype(F32)
        branch_ref[k] = wide_ref[:, :800].astype(BF16)
    mix_ref[...] = mixw_ref[...].astype(BF16)


def hold_kernel(src_ref, out_ref):
    del src_ref, out_ref


def project_kernel(emb_ref, emb_y_ref, *rest):
    w_refs, out_ref, acc_ref = rest[:-2], rest[-2], rest[-1]
    mine = lax.axis_index("yl")
    far_cut = w_refs[2].shape[0]
    tables, samples = emb_ref.shape[0], emb_ref.shape[1]
    free = lax.broadcasted_iota(jnp.int32, (samples, 128), 1) % 16 >= 12
    last = tables - 1
    extra = {}
    for t in [last] + list(range(last)):
        far = w_refs[2][t] if t < far_cut else w_refs[3][t - far_cut]
        weight = jnp.concatenate([w_refs[0][t], w_refs[1][t], far] + [ref[t] for ref in w_refs[4:]], axis=0)
        for k, ref in enumerate((emb_ref, emb_y_ref)):
            prod = nt_dot(ref[t], weight)
            if t == last:
                extra[k] = [jnp.where(free, pltpu.roll(prod, shift, 1), 0.0) for shift in (12, 8, 4)]
            else:
                if t < 3:
                    prod = prod + extra[k][t]
                slot = mine if k == 0 else 1 - mine
                acc_ref[slot, pl.ds(t, samples, stride=last), :] = prod
    for k in range(2):
        out_ref[k * samples : k * samples + samples] = acc_ref[k].reshape(samples, last, 128).astype(BF16)


def rows_kernel(recv_ref, weight_ref, mix_ref, fcot_ref, lcot_ref,
                fo_ref, lo_ref, keep_ref, send_ref, scr_ref, gt_ref, ft_ref, bf_ref, bl_ref):
    x, rep = lax.axis_index("x"), lax.axis_index("rep")
    place = lax.broadcasted_iota(jnp.int32, (32, 128), 1) % 16
    for yl in range(2):
        for tab in range(32):
            scr_ref[yl, 25 * tab : 25 * tab + 24, :] = recv_ref[yl * 32 + tab].astype(F32)
        last = [pltpu.roll(scr_ref[yl, pl.ds(k, 32, stride=25), :], 116 + 4 * k, 1) for k in range(3)]
        scr_ref[yl, pl.ds(24, 32, stride=25), :] = jnp.where(place < 4, last[0], jnp.where(place < 8, last[1], last[2]))
        gt_ref[yl] = scr_ref[yl].T
    for r in range(2):
        for yl in range(2):
            for spot in range(4):
                far = jnp.bitwise_xor(x, spot)
                start = pl.multiple_of((r + rep - 2 * r * rep) * 64 + far * 16, 16)
                row = r * 96 + yl * 48 + spot * 12
                ft_ref[row : row + 12, :] = gt_ref[yl, pl.ds(start, 16), :][:12]
    feat = ft_ref[...]
    feat_b = feat.astype(BF16)
    inner = nt_dot(mix_ref[...], feat_b)
    high = inner.astype(BF16)
    low = (inner - high.astype(F32)).astype(BF16)
    mixed_b = ((nn_dot(high, feat_b) + nn_dot(low, feat_b)) * (1.0 / 192)).astype(BF16)

    def branch(rows, weight, skip, cot_ref, out_ref, back_ref):
        pre = nt_dot(rows, weight) + skip
        inv = lax.rsqrt(jnp.sum(pre * pre, axis=0, keepdims=True) * (1.0 / 192) + EPS)
        normed = pre * inv
        out_ref[...] = normed.astype(BF16)
        cot = cot_ref[...].astype(F32)
        mean = jnp.sum(cot * normed, axis=0, keepdims=True) * (1.0 / 192)
        back = (inv * (cot - normed * mean)).T
        back_ref[...] = jnp.zeros_like(back_ref)
        for i in range(8):
            back_ref[56 * i : 56 * i + 50, :] = back[50 * i : 50 * i + 50]
        return back_ref[...].astype(BF16)

    back_l = branch(feat_b, weight_ref[1], ft_ref[:, 400:800], lcot_ref, lo_ref, bl_ref)
    back_f = branch(mixed_b, weight_ref[0], ft_ref[:, :400], fcot_ref, fo_ref, bf_ref)
    first = jnp.full((1, 1), rep, jnp.int32) == 0
    keep = nn_dot(jnp.where(first, back_f, back_l), jnp.where(first, mixed_b, feat_b))
    send = nn_dot(jnp.where(first, back_l, back_f), jnp.where(first, feat_b, mixed_b))
    for i in range(8):
        keep_ref[i] = keep[56 * i : 56 * i + 56].astype(BF16)
        send_ref[i] = send[56 * i : 56 * i + 56].astype(BF16)


def per_device(emb_rows, width_steps, proj_weight, fm_weight, lcb_weight, mix_weight, fm_cot, lcb_cot):
    tables, widest = emb_rows.shape[1], emb_rows.shape[2]
    emb = jnp.transpose(emb_rows, (1, 0, 2))
    emb_y = lax.ppermute(emb, "yl", SWAP)
    emb_y = pl.pallas_call(
        hold_kernel,
        out_shape=jax.ShapeDtypeStruct(emb.shape, BF16),
        in_specs=[pl.BlockSpec(memory_space=pl.ANY)],
        out_specs=pl.BlockSpec(memory_space=pl.ANY),
        input_output_aliases={0: 0},
        compiler_params=pltpu.CompilerParams(vmem_limit_bytes=1 << 20),
        cost_estimate=pl.CostEstimate(flops=20_000_000_000, bytes_accessed=0, transcendentals=0),
    )(emb_y)

    proj = jnp.transpose(proj_weight, (2, 0, 1))
    own, packed = pl.pallas_call(
        prep_kernel,
        out_shape=(
            jax.ShapeDtypeStruct((tables, 16, widest), BF16),
            jax.ShapeDtypeStruct((9, 56, 128), BF16),
        ),
        in_specs=[SM] + [pl.BlockSpec(memory_space=pl.ANY)] * 4,
        out_specs=(VM, VM),
        scratch_shapes=[
            pltpu.VMEM(proj.shape, BF16),
            pltpu.VMEM(fm_weight.shape, BF16),
            pltpu.VMEM(lcb_weight.shape, BF16),
            pltpu.VMEM(mix_weight.shape[::-1], BF16),
            pltpu.VMEM((4, 16 * tables, 128), F32),
            pltpu.SemaphoreType.DMA((4,)),
        ],
        cost_estimate=pl.CostEstimate(flops=1 << 20, bytes_accessed=2 << 20, transcendentals=0),
    )(width_steps, proj, fm_weight, lcb_weight, mix_weight.T)
    small = lax.all_gather(packed, ("rep", "yh", "yl", "x"), axis_index_groups=GROUPS)

    side, back = [(i, i ^ 1) for i in range(4)], [(i, i ^ 3) for i in range(4)]
    half = (tables + 1) // 2
    near = lax.ppermute(own, "x", side)
    next_ = lax.ppermute(own, "x", back)
    far_a = lax.ppermute(near[:half], "x", back)
    far_b = lax.ppermute(next_[half:], "x", side)
    far, emb_y = lax.optimization_barrier((jnp.concatenate([far_a, far_b], axis=0), emb_y))
    mine = [own, near, far_a, far_b, next_]
    other = [lax.ppermute(w, "rep", SWAP) for w in (own, near, far, next_)]

    chunks = call(
        project_kernel,
        jax.ShapeDtypeStruct((64, 24, 128), BF16),
        [emb, emb_y] + mine + other,
        [pltpu.VMEM((2, 768, 128), F32)],
        limit=SOME,
        flops=2 * 25 * 64 * 128 * 512,
        size=5 << 20,
    )
    recv = lax.all_to_all(chunks, ("yl",) + TAB, 0, 0, tiled=True)

    weights, mix_full = call(
        unpack_kernel,
        (jax.ShapeDtypeStruct((2, 400, 800), BF16), jax.ShapeDtypeStruct((192, 800), BF16)),
        [small],
        [pltpu.VMEM((400, 896), F32), pltpu.VMEM((192, 800), F32)],
        size=4 << 20,
        limit=SOME,
    )
    branch_out = jax.ShapeDtypeStruct((192, 400), BF16)
    partial = jax.ShapeDtypeStruct((8, 56, 800), BF16)
    fm_out, lcb_out, keep, send = call(
        rows_kernel,
        (branch_out, branch_out, partial, partial),
        [recv, weights, mix_full, fm_cot[0].T, lcb_cot[0].T],
        [
            pltpu.VMEM((2, 800, 128), F32),
            pltpu.VMEM((2, 128, 800), F32),
            pltpu.VMEM((192, 800), F32),
            pltpu.VMEM((448, 192), F32),
            pltpu.VMEM((448, 192), F32),
        ],
        limit=SOME,
        flops=700_000_000,
        size=5 << 20,
    )

    got = lax.ppermute(send, "rep", SWAP)
    pair = (keep.astype(F32) + got.astype(F32)).astype(BF16)
    shares = lax.all_to_all(pair, TP, 0, 0, tiled=True)
    share = jnp.sum(shares.astype(F32), axis=0).astype(BF16)
    share = jnp.pad(share, ((0, 8), (0, 224)))
    tiles = jnp.transpose(share.reshape(4, 16, 8, 128), (2, 0, 1, 3)).reshape(32, 16, 128)
    parts = lax.all_to_all(tiles, TAB, 0, 0, tiled=True)
    whole = jnp.sum(parts.astype(F32), axis=0).astype(BF16)
    spread = lax.all_to_all(jnp.broadcast_to(whole[None], (32, 16, 128)), TAB, 0, 0, tiled=True)
    swapped = lax.ppermute(spread, "rep", SWAP)

    def rows_of(blocks):
        wide = jnp.transpose(blocks.reshape(8, 4, 16, 128), (1, 2, 0, 3)).reshape(64, 1024)
        return wide[:50, :800].astype(F32)

    grad_a, grad_b = rows_of(spread), rows_of(swapped)
    first = lax.axis_index("rep") == 0
    grad_fm = jnp.where(first, grad_a, grad_b)
    grad_lcb = jnp.where(first, grad_b, grad_a)
    return fm_out.T[None], lcb_out.T[None], grad_fm, grad_lcb


def solution(mesh):
    fine = Mesh(mesh.devices.reshape(2, 8, 4, 2, 4), ("rep", "z", "yh", "yl", "x"))
    samples = ("rep", "yl", "x") + TAB
    in_specs = (
        P(("rep", "yl", "x"), TAB, None),
        P(TAB),
        P(TAB, None, ("rep", "yl", "x")),
        P(TP, None),
        P(TP, None),
        P(TP, None),
        P(samples, None, None),
        P(samples, None, None),
    )
    out_specs = (P(samples, None, None), P(samples, None, None), P(TP, None), P(TP, None))
    return jax.shard_map(per_device, mesh=fine, in_specs=in_specs, out_specs=out_specs, check_vma=False)
```

```python
import functools

import jax
import jax.numpy as jnp
from jax import lax
from jax.experimental import pallas as pl
from jax.experimental.pallas import tpu as pltpu
from jax.sharding import Mesh
from jax.sharding import PartitionSpec as P

F32 = jnp.float32
BF16 = jnp.bfloat16
EPS = 1e-06
SOME = 16 * 1024 * 1024
SWAP = [(0, 1), (1, 0)]
TAB = ("z", "yh")
TP = ("yl", "x")

VM = pl.BlockSpec(memory_space=pltpu.VMEM)
SM = pl.BlockSpec(memory_space=pltpu.SMEM)


def call(kernel, outs, ins, scratch=(), flops=0, size=0, limit=None):
    return pl.pallas_call(
        kernel,
        out_shape=outs,
        in_specs=[VM] * len(ins),
        out_specs=jax.tree.map(lambda _: VM, outs),
        scratch_shapes=list(scratch),
        compiler_params=pltpu.CompilerParams(vmem_limit_bytes=limit),
        cost_estimate=pl.CostEstimate(flops=flops, bytes_accessed=size, transcendentals=0),
    )(*ins)


def nt_dot(a, b):
    return lax.dot_general(a, b, (((1,), (1,)), ((), ())), preferred_element_type=F32)


def nn_dot(a, b):
    return lax.dot_general(a, b, (((1,), (0,)), ((), ())), preferred_element_type=F32)


def prep_kernel(steps_ref, proj_any, fm_any, lcb_any, mix_any, own_ref, pack_ref,
                proj_ref, fm_ref, lcb_ref, mix_ref, rows_ref, sems):
    copies = [
        pltpu.make_async_copy(src, dst, sems.at[k])
        for k, (src, dst) in enumerate(((proj_any, proj_ref), (fm_any, fm_ref), (lcb_any, lcb_ref), (mix_any, mix_ref)))
    ]
    for copy in copies:
        copy.start()
    tables, widest = proj_ref.shape[1], proj_ref.shape[2]
    columns = lax.broadcasted_iota(jnp.int32, (tables, widest), 1)
    table = lax.broadcasted_iota(jnp.int32, (tables, widest), 0)
    width = jnp.zeros((tables, widest), jnp.int32)
    for t in range(tables):
        width = jnp.where(table == t, steps_ref[t], width)
    keep = columns < widest // 8 * width
    rows_ref[...] = jnp.zeros_like(rows_ref)
    pack_ref[...] = jnp.zeros_like(pack_ref)
    copies[0].wait()
    for j in range(12):
        masked = jnp.where(keep, proj_ref[j].astype(F32), 0.0)
        for c in range(4):
            rows_ref[c, pl.ds(j, tables, stride=16), :] = masked[:, 128 * c : 128 * c + 128]
    for t in range(tables):
        for c in range(4):
            own_ref[t, :, 128 * c : 128 * c + 128] = rows_ref[c, 16 * t : 16 * t + 16, :].astype(BF16)
    for copy in copies[1:]:
        copy.wait()
    rep = lax.axis_index("rep")
    first = jnp.full((1, 1), rep, jnp.int32) == 0
    branch = jnp.where(first, fm_ref[...], lcb_ref[...])
    rows, cols = branch.shape
    for j in range(7):
        wide = min(128, cols - 128 * j)
        pack_ref[j, :rows, :wide] = branch[:, 128 * j : 128 * j + wide]
    for j in range(2):
        start = pl.multiple_of(rep * 96 + 48 * j, 16)
        pack_ref[7 + j, :48, : mix_ref.shape[1]] = mix_ref[pl.ds(start, 48), :]


def unpack_kernel(small_ref, branch_ref, mix_ref, wide_ref, mixw_ref):
    for k in range(2):
        for i in range(8):
            piece = small_ref.at[8 * k + i]
            for j in range(7):
                wide_ref[50 * i : 50 * i + 50, 128 * j : 128 * j + 128] = piece[j][:50].astype(F32)
            for j in range(2):
                row = 96 * k + 48 * j
                mixw_ref[row : row + 48, 100 * i : 100 * i + 100] = piece[7 + j][:48, :100].astype(F32)
        branch_ref[k] = wide_ref[:, :800].astype(BF16)
    mix_ref[...] = mixw_ref[...].astype(BF16)


def hold_kernel(src_ref, out_ref):
    del src_ref, out_ref


def project_kernel(emb_ref, emb_y_ref, *rest):
    w_refs, out_ref, acc_ref = rest[:-2], rest[-2], rest[-1]
    mine = lax.axis_index("yl")
    tables, samples = emb_ref.shape[0], emb_ref.shape[1]
    free = lax.broadcasted_iota(jnp.int32, (samples, 128), 1) % 16 >= 12
    last = tables - 1
    extra = {}
    for t in [last] + list(range(last)):
        weight = jnp.concatenate([ref[t] for ref in w_refs], axis=0)
        for k, ref in enumerate((emb_ref, emb_y_ref)):
            prod = nt_dot(ref[t], weight)
            if t == last:
                extra[k] = [jnp.where(free, pltpu.roll(prod, shift, 1), 0.0) for shift in (12, 8, 4)]
            else:
                if t < 3:
                    prod = prod + extra[k][t]
                slot = mine if k == 0 else 1 - mine
                acc_ref[slot, pl.ds(t, samples, stride=last), :] = prod
    for k in range(2):
        out_ref[k * samples : k * samples + samples] = acc_ref[k].reshape(samples, last, 128).astype(BF16)


def rows_kernel(recv_ref, weight_ref, mix_ref, fcot_ref, lcot_ref,
                fo_ref, lo_ref, keep_ref, send_ref, scr_ref, gt_ref, ft_ref, bf_ref, bl_ref):
    x, rep = lax.axis_index("x"), lax.axis_index("rep")
    place = lax.broadcasted_iota(jnp.int32, (32, 128), 1) % 16
    for yl in range(2):
        for tab in range(32):
            scr_ref[yl, 25 * tab : 25 * tab + 24, :] = recv_ref[yl * 32 + tab].astype(F32)
        last = [pltpu.roll(scr_ref[yl, pl.ds(k, 32, stride=25), :], 116 + 4 * k, 1) for k in range(3)]
        scr_ref[yl, pl.ds(24, 32, stride=25), :] = jnp.where(place < 4, last[0], jnp.where(place < 8, last[1], last[2]))
        gt_ref[yl] = scr_ref[yl].T
    for r in range(2):
        for yl in range(2):
            for spot in range(4):
                apart = jnp.bitwise_xor(x, spot)
                across = jnp.bitwise_xor(rep, r)
                side = jnp.where(apart == 1 + 2 * rep, 2 + across, 5 - across)
                block = jnp.where(apart == 0, across, jnp.where(apart == 2, 6 + across, side))
                start = pl.multiple_of(block * 16, 16)
                row = r * 96 + yl * 48 + spot * 12
                ft_ref[row : row + 12, :] = gt_ref[yl, pl.ds(start, 16), :][:12]
    feat = ft_ref[...]
    feat_b = feat.astype(BF16)
    inner = nt_dot(mix_ref[...], feat_b)
    high = inner.astype(BF16)
    low = (inner - high.astype(F32)).astype(BF16)
    mixed_b = ((nn_dot(high, feat_b) + nn_dot(low, feat_b)) * (1.0 / 192)).astype(BF16)

    def branch(rows, weight, skip, cot_ref, out_ref, back_ref):
        pre = nt_dot(rows, weight) + skip
        inv = lax.rsqrt(jnp.sum(pre * pre, axis=0, keepdims=True) * (1.0 / 192) + EPS)
        normed = pre * inv
        out_ref[...] = normed.astype(BF16)
        cot = cot_ref[...].astype(F32)
        mean = jnp.sum(cot * normed, axis=0, keepdims=True) * (1.0 / 192)
        back = (inv * (cot - normed * mean)).T
        back_ref[...] = jnp.zeros_like(back_ref)
        for i in range(8):
            back_ref[56 * i : 56 * i + 50, :] = back[50 * i : 50 * i + 50]
        return back_ref[...].astype(BF16)

    back_l = branch(feat_b, weight_ref[1], ft_ref[:, 400:800], lcot_ref, lo_ref, bl_ref)
    back_f = branch(mixed_b, weight_ref[0], ft_ref[:, :400], fcot_ref, fo_ref, bf_ref)
    first = jnp.full((1, 1), rep, jnp.int32) == 0
    keep = nn_dot(jnp.where(first, back_f, back_l), jnp.where(first, mixed_b, feat_b))
    send = nn_dot(jnp.where(first, back_l, back_f), jnp.where(first, feat_b, mixed_b))
    for i in range(8):
        keep_ref[i] = keep[56 * i : 56 * i + 56].astype(BF16)
        send_ref[i] = send[56 * i : 56 * i + 56].astype(BF16)


def per_device(emb_rows, width_steps, proj_weight, fm_weight, lcb_weight, mix_weight, fm_cot, lcb_cot):
    tables, widest = emb_rows.shape[1], emb_rows.shape[2]
    emb = jnp.transpose(emb_rows, (1, 0, 2))
    emb_y = lax.ppermute(emb, "yl", SWAP)
    emb_y = pl.pallas_call(
        hold_kernel,
        out_shape=jax.ShapeDtypeStruct(emb.shape, BF16),
        in_specs=[pl.BlockSpec(memory_space=pl.ANY)],
        out_specs=pl.BlockSpec(memory_space=pl.ANY),
        input_output_aliases={0: 0},
        compiler_params=pltpu.CompilerParams(vmem_limit_bytes=1 << 20),
        cost_estimate=pl.CostEstimate(flops=20_000_000_000, bytes_accessed=0, transcendentals=0),
    )(emb_y)

    proj = jnp.transpose(proj_weight, (2, 0, 1))
    own, packed = pl.pallas_call(
        prep_kernel,
        out_shape=(
            jax.ShapeDtypeStruct((tables, 16, widest), BF16),
            jax.ShapeDtypeStruct((9, 56, 128), BF16),
        ),
        in_specs=[SM] + [pl.BlockSpec(memory_space=pl.ANY)] * 4,
        out_specs=(VM, VM),
        scratch_shapes=[
            pltpu.VMEM(proj.shape, BF16),
            pltpu.VMEM(fm_weight.shape, BF16),
            pltpu.VMEM(lcb_weight.shape, BF16),
            pltpu.VMEM(mix_weight.shape[::-1], BF16),
            pltpu.VMEM((4, 16 * tables, 128), F32),
            pltpu.SemaphoreType.DMA((4,)),
        ],
        cost_estimate=pl.CostEstimate(flops=1 << 20, bytes_accessed=2 << 20, transcendentals=0),
    )(width_steps, proj, fm_weight, lcb_weight, mix_weight.T)
    small = lax.all_gather(packed, ("rep",) + TP)

    side = [(4 * rep + x, 4 * rep + (x ^ (1, 3)[rep])) for rep in range(2) for x in range(4)]
    onward = [(4 * rep + x, 4 * rep + (x ^ (3, 1)[rep])) for rep in range(2) for x in range(4)]
    near_a = lax.ppermute(own, ("rep", "x"), side)
    own_o = lax.ppermute(own, "rep", SWAP)
    near_b = lax.ppermute(own_o, ("rep", "x"), side)
    far = lax.ppermute(near_a, ("rep", "x"), onward)
    next_a = lax.ppermute(near_a, "rep", SWAP)
    far_o = lax.ppermute(far, "rep", SWAP)
    near_b, emb_y = lax.optimization_barrier((near_b, emb_y))
    next_b = lax.ppermute(near_b, "rep", SWAP)

    chunks = call(
        project_kernel,
        jax.ShapeDtypeStruct((64, 24, 128), BF16),
        [emb, emb_y, own, own_o, near_a, near_b, next_a, next_b, far, far_o],
        [pltpu.VMEM((2, 768, 128), F32)],
        limit=SOME,
        flops=2 * 25 * 64 * 128 * 512,
        size=5 << 20,
    )
    recv = lax.all_to_all(chunks, ("yl",) + TAB, 0, 0, tiled=True)

    weights, mix_full = call(
        unpack_kernel,
        (jax.ShapeDtypeStruct((2, 400, 800), BF16), jax.ShapeDtypeStruct((192, 800), BF16)),
        [small],
        [pltpu.VMEM((400, 896), F32), pltpu.VMEM((192, 800), F32)],
        size=4 << 20,
        limit=SOME,
    )
    branch_out = jax.ShapeDtypeStruct((192, 400), BF16)
    partial = jax.ShapeDtypeStruct((8, 56, 800), BF16)
    fm_out, lcb_out, keep, send = call(
        rows_kernel,
        (branch_out, branch_out, partial, partial),
        [recv, weights, mix_full, fm_cot[0].T, lcb_cot[0].T],
        [
            pltpu.VMEM((2, 800, 128), F32),
            pltpu.VMEM((2, 128, 800), F32),
            pltpu.VMEM((192, 800), F32),
            pltpu.VMEM((448, 192), F32),
            pltpu.VMEM((448, 192), F32),
        ],
        limit=SOME,
        flops=700_000_000,
        size=5 << 20,
    )

    got = lax.ppermute(send, "rep", SWAP)
    pair = (keep.astype(F32) + got.astype(F32)).astype(BF16)
    shares = lax.all_to_all(pair, TP, 0, 0, tiled=True)
    share = jnp.sum(shares.astype(F32), axis=0).astype(BF16)
    share = jnp.pad(share, ((0, 8), (0, 224)))
    tiles = jnp.transpose(share.reshape(4, 16, 8, 128), (2, 0, 1, 3)).reshape(32, 16, 128)
    parts = lax.all_to_all(tiles, TAB, 0, 0, tiled=True)
    whole = jnp.sum(parts.astype(F32), axis=0).astype(BF16)
    spread = lax.all_to_all(jnp.broadcast_to(whole[None], (32, 16, 128)), TAB, 0, 0, tiled=True)
    swapped = lax.ppermute(spread, "rep", SWAP)

    def rows_of(blocks):
        wide = jnp.transpose(blocks.reshape(8, 4, 16, 128), (1, 2, 0, 3)).reshape(64, 1024)
        return wide[:50, :800].astype(F32)

    grad_a, grad_b = rows_of(spread), rows_of(swapped)
    first = lax.axis_index("rep") == 0
    grad_fm = jnp.where(first, grad_a, grad_b)
    grad_lcb = jnp.where(first, grad_b, grad_a)
    return fm_out.T[None], lcb_out.T[None], grad_fm, grad_lcb


def solution(mesh):
    fine = Mesh(mesh.devices.reshape(2, 8, 4, 2, 4), ("rep", "z", "yh", "yl", "x"))
    samples = ("rep", "yl", "x") + TAB
    in_specs = (
        P(("rep", "yl", "x"), TAB, None),
        P(TAB),
        P(TAB, None, ("rep", "yl", "x")),
        P(TP, None),
        P(TP, None),
        P(TP, None),
        P(samples, None, None),
        P(samples, None, None),
    )
    out_specs = (P(samples, None, None), P(samples, None, None), P(TP, None), P(TP, None))
    return jax.shard_map(per_device, mesh=fine, in_specs=in_specs, out_specs=out_specs, check_vma=False)
```

```python
import functools

import jax
import jax.numpy as jnp
from jax import lax
from jax.experimental import pallas as pl
from jax.experimental.pallas import tpu as pltpu
from jax.sharding import Mesh
from jax.sharding import PartitionSpec as P

F32 = jnp.float32
BF16 = jnp.bfloat16
EPS = 1e-06
SOME = 16 * 1024 * 1024
SWAP = [(0, 1), (1, 0)]
TAB = ("z", "yh")
TP = ("yl", "x")

VM = pl.BlockSpec(memory_space=pltpu.VMEM)
SM = pl.BlockSpec(memory_space=pltpu.SMEM)


def call(kernel, outs, ins, scratch=(), flops=0, size=0, limit=None):
    return pl.pallas_call(
        kernel,
        out_shape=outs,
        in_specs=[VM] * len(ins),
        out_specs=jax.tree.map(lambda _: VM, outs),
        scratch_shapes=list(scratch),
        compiler_params=pltpu.CompilerParams(vmem_limit_bytes=limit),
        cost_estimate=pl.CostEstimate(flops=flops, bytes_accessed=size, transcendentals=0),
    )(*ins)


def nt_dot(a, b):
    return lax.dot_general(a, b, (((1,), (1,)), ((), ())), preferred_element_type=F32)


def nn_dot(a, b):
    return lax.dot_general(a, b, (((1,), (0,)), ((), ())), preferred_element_type=F32)


def prep_kernel(steps_ref, proj_any, fm_any, lcb_any, mix_any, own_ref, pack_ref,
                proj_ref, fm_ref, lcb_ref, mix_ref, rows_ref, sems):
    copies = [
        pltpu.make_async_copy(src, dst, sems.at[k])
        for k, (src, dst) in enumerate(((proj_any, proj_ref), (fm_any, fm_ref), (lcb_any, lcb_ref), (mix_any, mix_ref)))
    ]
    for copy in copies:
        copy.start()
    tables, widest = proj_ref.shape[1], proj_ref.shape[2]
    columns = lax.broadcasted_iota(jnp.int32, (tables, widest), 1)
    table = lax.broadcasted_iota(jnp.int32, (tables, widest), 0)
    width = jnp.zeros((tables, widest), jnp.int32)
    for t in range(tables):
        width = jnp.where(table == t, steps_ref[t], width)
    keep = columns < widest // 8 * width
    rows_ref[...] = jnp.zeros_like(rows_ref)
    pack_ref[...] = jnp.zeros_like(pack_ref)
    copies[0].wait()
    for j in range(12):
        masked = jnp.where(keep, proj_ref[j].astype(F32), 0.0)
        for c in range(4):
            rows_ref[c, pl.ds(j, tables, stride=16), :] = masked[:, 128 * c : 128 * c + 128]
    for t in range(tables):
        for c in range(4):
            own_ref[t, :, 128 * c : 128 * c + 128] = rows_ref[c, 16 * t : 16 * t + 16, :].astype(BF16)
    for copy in copies[1:]:
        copy.wait()
    rep = lax.axis_index("rep")
    first = jnp.full((1, 1), rep, jnp.int32) == 0
    branch = jnp.where(first, fm_ref[...], lcb_ref[...])
    rows, cols = branch.shape
    for j in range(7):
        wide = min(128, cols - 128 * j)
        pack_ref[j, :rows, :wide] = branch[:, 128 * j : 128 * j + wide]
    for j in range(2):
        start = pl.multiple_of(rep * 96 + 48 * j, 16)
        pack_ref[7 + j, :48, : mix_ref.shape[1]] = mix_ref[pl.ds(start, 48), :]


def unpack_kernel(small_ref, branch_ref, mix_ref, wide_ref, mixw_ref):
    for k in range(2):
        for i in range(8):
            piece = small_ref.at[8 * k + i]
            for j in range(7):
                wide_ref[50 * i : 50 * i + 50, 128 * j : 128 * j + 128] = piece[j][:50].astype(F32)
            for j in range(2):
                row = 96 * k + 48 * j
                mixw_ref[row : row + 48, 100 * i : 100 * i + 100] = piece[7 + j][:48, :100].astype(F32)
        branch_ref[k] = wide_ref[:, :800].astype(BF16)
    mix_ref[...] = mixw_ref[...].astype(BF16)


def hold_kernel(src_ref, out_ref):
    del src_ref, out_ref


def project_kernel(emb_ref, emb_y_ref, *rest):
    w_refs, out_ref, acc_ref = rest[:-2], rest[-2], rest[-1]
    mine = lax.axis_index("yl")
    own_ref, near_refs, far_refs, next_refs, other_refs = w_refs[0], w_refs[1:3], w_refs[3:5], w_refs[5:7], w_refs[7:]
    half = near_refs[0].shape[0]
    tables, samples = emb_ref.shape[0], emb_ref.shape[1]
    free = lax.broadcasted_iota(jnp.int32, (samples, 128), 1) % 16 >= 12
    last = tables - 1
    extra = {}
    for t in [last] + list(range(last)):
        part, row = (0, t) if t < half else (1, t - half)
        blocks = [own_ref[t]] + [refs[part][row] for refs in (near_refs, far_refs, next_refs)]
        blocks += [other_refs[0][t], other_refs[1][0, t], other_refs[2][t], other_refs[1][1, t]]
        weight = jnp.concatenate(blocks, axis=0)
        for k, ref in enumerate((emb_ref, emb_y_ref)):
            prod = nt_dot(ref[t], weight)
            if t == last:
                extra[k] = [jnp.where(free, pltpu.roll(prod, shift, 1), 0.0) for shift in (12, 8, 4)]
            else:
                if t < 3:
                    prod = prod + extra[k][t]
                slot = mine if k == 0 else 1 - mine
                acc_ref[slot, pl.ds(t, samples, stride=last), :] = prod
    for k in range(2):
        out_ref[k * samples : k * samples + samples] = acc_ref[k].reshape(samples, last, 128).astype(BF16)


def rows_kernel(recv_ref, weight_ref, mix_ref, fcot_ref, lcot_ref,
                fo_ref, lo_ref, keep_ref, send_ref, scr_ref, gt_ref, ft_ref, bf_ref, bl_ref):
    x, rep = lax.axis_index("x"), lax.axis_index("rep")
    place = lax.broadcasted_iota(jnp.int32, (32, 128), 1) % 16
    for yl in range(2):
        for tab in range(32):
            scr_ref[yl, 25 * tab : 25 * tab + 24, :] = recv_ref[yl * 32 + tab].astype(F32)
        last = [pltpu.roll(scr_ref[yl, pl.ds(k, 32, stride=25), :], 116 + 4 * k, 1) for k in range(3)]
        scr_ref[yl, pl.ds(24, 32, stride=25), :] = jnp.where(place < 4, last[0], jnp.where(place < 8, last[1], last[2]))
        gt_ref[yl] = scr_ref[yl].T
    for r in range(2):
        for yl in range(2):
            for spot in range(4):
                far = jnp.bitwise_xor(x, spot)
                start = pl.multiple_of((r + rep - 2 * r * rep) * 64 + far * 16, 16)
                row = r * 96 + yl * 48 + spot * 12
                ft_ref[row : row + 12, :] = gt_ref[yl, pl.ds(start, 16), :][:12]
    feat = ft_ref[...]
    feat_b = feat.astype(BF16)
    inner = nt_dot(mix_ref[...], feat_b)
    high = inner.astype(BF16)
    low = (inner - high.astype(F32)).astype(BF16)
    mixed_b = ((nn_dot(high, feat_b) + nn_dot(low, feat_b)) * (1.0 / 192)).astype(BF16)

    def branch(rows, weight, skip, cot_ref, out_ref, back_ref):
        pre = nt_dot(rows, weight) + skip
        inv = lax.rsqrt(jnp.sum(pre * pre, axis=0, keepdims=True) * (1.0 / 192) + EPS)
        normed = pre * inv
        out_ref[...] = normed.astype(BF16)
        cot = cot_ref[...].astype(F32)
        mean = jnp.sum(cot * normed, axis=0, keepdims=True) * (1.0 / 192)
        back = (inv * (cot - normed * mean)).T
        back_ref[...] = jnp.zeros_like(back_ref)
        for i in range(8):
            back_ref[56 * i : 56 * i + 50, :] = back[50 * i : 50 * i + 50]
        return back_ref[...].astype(BF16)

    back_l = branch(feat_b, weight_ref[1], ft_ref[:, 400:800], lcot_ref, lo_ref, bl_ref)
    back_f = branch(mixed_b, weight_ref[0], ft_ref[:, :400], fcot_ref, fo_ref, bf_ref)
    first = jnp.full((1, 1), rep, jnp.int32) == 0
    keep = nn_dot(jnp.where(first, back_f, back_l), jnp.where(first, mixed_b, feat_b))
    send = nn_dot(jnp.where(first, back_l, back_f), jnp.where(first, feat_b, mixed_b))
    for i in range(8):
        keep_ref[i] = keep[56 * i : 56 * i + 56].astype(BF16)
        send_ref[i] = send[56 * i : 56 * i + 56].astype(BF16)


def per_device(emb_rows, width_steps, proj_weight, fm_weight, lcb_weight, mix_weight, fm_cot, lcb_cot):
    tables, widest = emb_rows.shape[1], emb_rows.shape[2]
    emb = jnp.transpose(emb_rows, (1, 0, 2))
    emb_y = lax.ppermute(emb, "yl", SWAP)
    emb_y = pl.pallas_call(
        hold_kernel,
        out_shape=jax.ShapeDtypeStruct(emb.shape, BF16),
        in_specs=[pl.BlockSpec(memory_space=pl.ANY)],
        out_specs=pl.BlockSpec(memory_space=pl.ANY),
        input_output_aliases={0: 0},
        compiler_params=pltpu.CompilerParams(vmem_limit_bytes=1 << 20),
        cost_estimate=pl.CostEstimate(flops=20_000_000_000, bytes_accessed=0, transcendentals=0),
    )(emb_y)

    proj = jnp.transpose(proj_weight, (2, 0, 1))
    own, packed = pl.pallas_call(
        prep_kernel,
        out_shape=(
            jax.ShapeDtypeStruct((tables, 16, widest), BF16),
            jax.ShapeDtypeStruct((9, 56, 128), BF16),
        ),
        in_specs=[SM] + [pl.BlockSpec(memory_space=pl.ANY)] * 4,
        out_specs=(VM, VM),
        scratch_shapes=[
            pltpu.VMEM(proj.shape, BF16),
            pltpu.VMEM(fm_weight.shape, BF16),
            pltpu.VMEM(lcb_weight.shape, BF16),
            pltpu.VMEM(mix_weight.shape[::-1], BF16),
            pltpu.VMEM((4, 16 * tables, 128), F32),
            pltpu.SemaphoreType.DMA((4,)),
        ],
        cost_estimate=pl.CostEstimate(flops=1 << 20, bytes_accessed=2 << 20, transcendentals=0),
    )(width_steps, proj, fm_weight, lcb_weight, mix_weight.T)
    small = lax.all_gather(packed, ("rep",) + TP)

    side, back = [(i, i ^ 1) for i in range(4)], [(i, i ^ 3) for i in range(4)]
    half = (tables + 1) // 2
    own_a, own_b = own[:half], own[half:]
    near_a = lax.ppermute(own_a, "x", side)
    next_b = lax.ppermute(own_b, "x", back)
    near_b = lax.ppermute(own_b, "x", side)
    next_a = lax.ppermute(own_a, "x", back)
    far_a = lax.ppermute(near_a, "x", back)
    far_b = lax.ppermute(next_b, "x", side)
    far = [far_a, far_b]
    near = [near_a, near_b]
    next_ = [next_a, next_b]
    far_w, emb_y = lax.optimization_barrier((jnp.concatenate(far, axis=0), emb_y))
    beside = jnp.stack([jnp.concatenate(near, axis=0), jnp.concatenate(next_, axis=0)])
    other = [lax.ppermute(w, "rep", SWAP) for w in (own, beside, far_w)]

    chunks = call(
        project_kernel,
        jax.ShapeDtypeStruct((64, 24, 128), BF16),
        [emb, emb_y, own] + near + far + next_ + other,
        [pltpu.VMEM((2, 768, 128), F32)],
        limit=SOME,
        flops=2 * 25 * 64 * 128 * 512,
        size=5 << 20,
    )
    recv = lax.all_to_all(chunks, ("yl",) + TAB, 0, 0, tiled=True)

    weights, mix_full = call(
        unpack_kernel,
        (jax.ShapeDtypeStruct((2, 400, 800), BF16), jax.ShapeDtypeStruct((192, 800), BF16)),
        [small],
        [pltpu.VMEM((400, 896), F32), pltpu.VMEM((192, 800), F32)],
        size=4 << 20,
        limit=SOME,
    )
    branch_out = jax.ShapeDtypeStruct((192, 400), BF16)
    partial = jax.ShapeDtypeStruct((8, 56, 800), BF16)
    fm_out, lcb_out, keep, send = call(
        rows_kernel,
        (branch_out, branch_out, partial, partial),
        [recv, weights, mix_full, fm_cot[0].T, lcb_cot[0].T],
        [
            pltpu.VMEM((2, 800, 128), F32),
            pltpu.VMEM((2, 128, 800), F32),
            pltpu.VMEM((192, 800), F32),
            pltpu.VMEM((448, 192), F32),
            pltpu.VMEM((448, 192), F32),
        ],
        limit=SOME,
        flops=700_000_000,
        size=5 << 20,
    )

    got = lax.ppermute(send, "rep", SWAP)
    pair = (keep.astype(F32) + got.astype(F32)).astype(BF16)
    shares = lax.all_to_all(pair, TP, 0, 0, tiled=True)
    share = jnp.sum(shares.astype(F32), axis=0).astype(BF16)
    share = jnp.pad(share, ((0, 8), (0, 224)))
    tiles = jnp.transpose(share.reshape(4, 16, 8, 128), (2, 0, 1, 3)).reshape(32, 16, 128)
    parts = lax.all_to_all(tiles, TAB, 0, 0, tiled=True)
    whole = jnp.sum(parts.astype(F32), axis=0).astype(BF16)
    spread = lax.all_to_all(jnp.broadcast_to(whole[None], (32, 16, 128)), TAB, 0, 0, tiled=True)
    swapped = lax.ppermute(spread, "rep", SWAP)

    def rows_of(blocks):
        wide = jnp.transpose(blocks.reshape(8, 4, 16, 128), (1, 2, 0, 3)).reshape(64, 1024)
        return wide[:50, :800].astype(F32)

    grad_a, grad_b = rows_of(spread), rows_of(swapped)
    first = lax.axis_index("rep") == 0
    grad_fm = jnp.where(first, grad_a, grad_b)
    grad_lcb = jnp.where(first, grad_b, grad_a)
    return fm_out.T[None], lcb_out.T[None], grad_fm, grad_lcb


def solution(mesh):
    fine = Mesh(mesh.devices.reshape(2, 8, 4, 2, 4), ("rep", "z", "yh", "yl", "x"))
    samples = ("rep", "yl", "x") + TAB
    in_specs = (
        P(("rep", "yl", "x"), TAB, None),
        P(TAB),
        P(TAB, None, ("rep", "yl", "x")),
        P(TP, None),
        P(TP, None),
        P(TP, None),
        P(samples, None, None),
        P(samples, None, None),
    )
    out_specs = (P(samples, None, None), P(samples, None, None), P(TP, None), P(TP, None))
    return jax.shard_map(per_device, mesh=fine, in_specs=in_specs, out_specs=out_specs, check_vma=False)
```

```python
import functools

import jax
import jax.numpy as jnp
from jax import lax
from jax.experimental import pallas as pl
from jax.experimental.pallas import tpu as pltpu
from jax.sharding import Mesh
from jax.sharding import PartitionSpec as P

F32 = jnp.float32
BF16 = jnp.bfloat16
EPS = 1e-06
SOME = 16 * 1024 * 1024
SWAP = [(0, 1), (1, 0)]
TAB = ("z", "yh")
TP = ("yl", "x")

VM = pl.BlockSpec(memory_space=pltpu.VMEM)
SM = pl.BlockSpec(memory_space=pltpu.SMEM)


def call(kernel, outs, ins, scratch=(), flops=0, size=0, limit=None):
    return pl.pallas_call(
        kernel,
        out_shape=outs,
        in_specs=[VM] * len(ins),
        out_specs=jax.tree.map(lambda _: VM, outs),
        scratch_shapes=list(scratch),
        compiler_params=pltpu.CompilerParams(vmem_limit_bytes=limit),
        cost_estimate=pl.CostEstimate(flops=flops, bytes_accessed=size, transcendentals=0),
    )(*ins)


def nt_dot(a, b):
    return lax.dot_general(a, b, (((1,), (1,)), ((), ())), preferred_element_type=F32)


def nn_dot(a, b):
    return lax.dot_general(a, b, (((1,), (0,)), ((), ())), preferred_element_type=F32)


def prep_kernel(steps_ref, proj_any, fm_any, lcb_any, mix_any, own_ref, pack_ref,
                proj_ref, fm_ref, lcb_ref, mix_ref, rows_ref, sems):
    copies = [
        pltpu.make_async_copy(src, dst, sems.at[k])
        for k, (src, dst) in enumerate(((proj_any, proj_ref), (fm_any, fm_ref), (lcb_any, lcb_ref), (mix_any, mix_ref)))
    ]
    for copy in copies:
        copy.start()
    tables, widest = proj_ref.shape[1], proj_ref.shape[2]
    columns = lax.broadcasted_iota(jnp.int32, (tables, widest), 1)
    table = lax.broadcasted_iota(jnp.int32, (tables, 128), 0)
    width = jnp.zeros((tables, 128), jnp.int32)
    for t in range(tables):
        width = jnp.where(table == t, widest // 8 * steps_ref[t], width)
    keep = columns < jnp.concatenate([width] * (widest // 128), axis=1)
    rows_ref[...] = jnp.zeros_like(rows_ref)
    pack_ref[...] = jnp.zeros_like(pack_ref)
    copies[0].wait()
    for j in range(12):
        masked = jnp.where(keep, proj_ref[j].astype(F32), 0.0)
        for c in range(4):
            rows_ref[c, pl.ds(j, tables, stride=12), :] = masked[:, 128 * c : 128 * c + 128]
    for p in range(own_ref.shape[0]):
        for c in range(4):
            own_ref[p, :, 128 * c : 128 * c + 128] = rows_ref[c, 24 * p : 24 * p + 24, :].astype(BF16)
    for copy in copies[1:]:
        copy.wait()
    rep = lax.axis_index("rep")
    first = jnp.full((1, 1), rep, jnp.int32) == 0
    branch = jnp.where(first, fm_ref[...], lcb_ref[...])
    rows, cols = branch.shape
    for j in range(7):
        wide = min(128, cols - 128 * j)
        pack_ref[j, :rows, :wide] = branch[:, 128 * j : 128 * j + wide]
    for j in range(2):
        start = pl.multiple_of(rep * 96 + 48 * j, 16)
        pack_ref[7 + j, :48, : mix_ref.shape[1]] = mix_ref[pl.ds(start, 48), :]


def unpack_kernel(small_ref, branch_ref, mix_ref, wide_ref, mixw_ref):
    for k in range(2):
        for i in range(8):
            piece = small_ref.at[8 * k + i]
            for j in range(7):
                wide_ref[50 * i : 50 * i + 50, 128 * j : 128 * j + 128] = piece[j][:50].astype(F32)
            for j in range(2):
                row = 96 * k + 48 * j
                mixw_ref[row : row + 48, 100 * i : 100 * i + 100] = piece[7 + j][:48, :100].astype(F32)
        branch_ref[k] = wide_ref[:, :800].astype(BF16)
    mix_ref[...] = mixw_ref[...].astype(BF16)


def hold_kernel(src_ref, out_ref):
    del src_ref, out_ref


def project_kernel(emb_ref, emb_y_ref, *rest):
    w_refs, out_ref, acc_ref = rest[:-2], rest[-2], rest[-1]
    mine = lax.axis_index("yl")
    far_cut = w_refs[2].shape[0]
    tables, samples = emb_ref.shape[0], emb_ref.shape[1]
    free = lax.broadcasted_iota(jnp.int32, (samples, 128), 1) % 16 >= 12
    last = tables - 1
    extra = {}
    for t in [last] + list(range(last)):
        pair, odd = t // 2, t % 2
        far = w_refs[2].at[pair] if pair < far_cut else w_refs[3].at[pair - far_cut]
        blocks = [w_refs[0].at[pair], w_refs[1].at[pair], far] + [ref.at[pair] for ref in w_refs[4:]]
        weight = jnp.concatenate([block[8 * odd : 8 * odd + 16, :] for block in blocks], axis=0)
        for k, ref in enumerate((emb_ref, emb_y_ref)):
            prod = nt_dot(ref[t], weight)
            if odd:
                prod = pltpu.roll(prod, 124, 1)
            if t == last:
                extra[k] = [pltpu.roll(prod, shift, 1) for shift in (12, 8, 4)]
            else:
                prod = jnp.where(free, extra[k][t] if t < 3 else 0.0, prod)
                slot = mine if k == 0 else 1 - mine
                acc_ref[slot, pl.ds(t, samples, stride=last), :] = prod
    for k in range(2):
        out_ref[k * samples : k * samples + samples] = acc_ref[k].reshape(samples, last, 128).astype(BF16)


def rows_kernel(recv_ref, weight_ref, mix_ref, fcot_ref, lcot_ref,
                fo_ref, lo_ref, keep_ref, send_ref, scr_ref, gt_ref, ft_ref, bf_ref, bl_ref):
    x, rep = lax.axis_index("x"), lax.axis_index("rep")
    place = lax.broadcasted_iota(jnp.int32, (32, 128), 1) % 16
    for yl in range(2):
        for tab in range(32):
            scr_ref[yl, 25 * tab : 25 * tab + 24, :] = recv_ref[yl * 32 + tab].astype(F32)
        last = [pltpu.roll(scr_ref[yl, pl.ds(k, 32, stride=25), :], 116 + 4 * k, 1) for k in range(3)]
        scr_ref[yl, pl.ds(24, 32, stride=25), :] = jnp.where(place < 4, last[0], jnp.where(place < 8, last[1], last[2]))
        gt_ref[yl] = scr_ref[yl].T
    for r in range(2):
        for yl in range(2):
            for spot in range(4):
                far = jnp.bitwise_xor(x, spot)
                start = pl.multiple_of((r + rep - 2 * r * rep) * 64 + far * 16, 16)
                row = r * 96 + yl * 48 + spot * 12
                ft_ref[row : row + 12, :] = gt_ref[yl, pl.ds(start, 16), :][:12]
    feat = ft_ref[...]
    feat_b = feat.astype(BF16)
    inner = nt_dot(mix_ref[...], feat_b)
    high = inner.astype(BF16)
    low = (inner - high.astype(F32)).astype(BF16)
    mixed_b = ((nn_dot(high, feat_b) + nn_dot(low, feat_b)) * (1.0 / 192)).astype(BF16)

    def branch(rows, weight, skip, cot_ref, out_ref, back_ref):
        pre = nt_dot(rows, weight) + skip
        inv = lax.rsqrt(jnp.sum(pre * pre, axis=0, keepdims=True) * (1.0 / 192) + EPS)
        normed = pre * inv
        out_ref[...] = normed.astype(BF16)
        cot = cot_ref[...].astype(F32)
        mean = jnp.sum(cot * normed, axis=0, keepdims=True) * (1.0 / 192)
        back = (inv * (cot - normed * mean)).T
        back_ref[...] = jnp.zeros_like(back_ref)
        for i in range(8):
            back_ref[56 * i : 56 * i + 50, :] = back[50 * i : 50 * i + 50]
        return back_ref[...].astype(BF16)

    back_l = branch(feat_b, weight_ref[1], ft_ref[:, 400:800], lcot_ref, lo_ref, bl_ref)
    back_f = branch(mixed_b, weight_ref[0], ft_ref[:, :400], fcot_ref, fo_ref, bf_ref)
    first = jnp.full((1, 1), rep, jnp.int32) == 0
    keep = nn_dot(jnp.where(first, back_f, back_l), jnp.where(first, mixed_b, feat_b))
    send = nn_dot(jnp.where(first, back_l, back_f), jnp.where(first, feat_b, mixed_b))
    for i in range(8):
        keep_ref[i] = keep[56 * i : 56 * i + 56].astype(BF16)
        send_ref[i] = send[56 * i : 56 * i + 56].astype(BF16)


def per_device(emb_rows, width_steps, proj_weight, fm_weight, lcb_weight, mix_weight, fm_cot, lcb_cot):
    tables, widest = emb_rows.shape[1], emb_rows.shape[2]
    emb = jnp.transpose(emb_rows, (1, 0, 2))
    emb_y = lax.ppermute(emb, "yl", SWAP)
    emb_y = pl.pallas_call(
        hold_kernel,
        out_shape=jax.ShapeDtypeStruct(emb.shape, BF16),
        in_specs=[pl.BlockSpec(memory_space=pl.ANY)],
        out_specs=pl.BlockSpec(memory_space=pl.ANY),
        input_output_aliases={0: 0},
        compiler_params=pltpu.CompilerParams(vmem_limit_bytes=1 << 20),
        cost_estimate=pl.CostEstimate(flops=30_000_000_000, bytes_accessed=0, transcendentals=0),
    )(emb_y)

    pairs = (tables + 1) // 2
    proj = jnp.transpose(proj_weight, (2, 0, 1))
    own, packed = pl.pallas_call(
        prep_kernel,
        out_shape=(
            jax.ShapeDtypeStruct((pairs, 24, widest), BF16),
            jax.ShapeDtypeStruct((9, 56, 128), BF16),
        ),
        in_specs=[SM] + [pl.BlockSpec(memory_space=pl.ANY)] * 4,
        out_specs=(VM, VM),
        scratch_shapes=[
            pltpu.VMEM(proj.shape, BF16),
            pltpu.VMEM(fm_weight.shape, BF16),
            pltpu.VMEM(lcb_weight.shape, BF16),
            pltpu.VMEM(mix_weight.shape[::-1], BF16),
            pltpu.VMEM((4, 24 * pairs, 128), F32),
            pltpu.SemaphoreType.DMA((4,)),
        ],
        cost_estimate=pl.CostEstimate(flops=1 << 20, bytes_accessed=2 << 20, transcendentals=0),
    )(width_steps, proj, fm_weight, lcb_weight, mix_weight.T)
    small = lax.all_gather(packed, ("rep",) + TP)

    side, back = [(i, i ^ 1) for i in range(4)], [(i, i ^ 3) for i in range(4)]
    half = (pairs + 1) // 2
    near = lax.ppermute(own, "x", side)
    next_ = lax.ppermute(own, "x", back)
    own_o = lax.ppermute(own, "rep", SWAP)
    near, own_o = lax.optimization_barrier((near, own_o))
    far_a = lax.ppermute(near[:half], "x", back)
    far_b = lax.ppermute(next_[half:], "x", side)
    near_o = lax.ppermute(near, "rep", SWAP)
    next_o = lax.ppermute(next_, "rep", SWAP)
    far, emb_y = lax.optimization_barrier((jnp.concatenate([far_a, far_b], axis=0), emb_y))
    far_o = lax.ppermute(far, "rep", SWAP)
    mine = [own, near, far_a, far_b, next_]
    other = [own_o, near_o, far_o, next_o]

    chunks = call(
        project_kernel,
        jax.ShapeDtypeStruct((64, 24, 128), BF16),
        [emb, emb_y] + mine + other,
        [pltpu.VMEM((2, 768, 128), F32)],
        limit=SOME,
        flops=2 * 25 * 64 * 128 * 512,
        size=5 << 20,
    )
    recv = lax.all_to_all(chunks, ("yl",) + TAB, 0, 0, tiled=True)

    weights, mix_full = call(
        unpack_kernel,
        (jax.ShapeDtypeStruct((2, 400, 800), BF16), jax.ShapeDtypeStruct((192, 800), BF16)),
        [small],
        [pltpu.VMEM((400, 896), F32), pltpu.VMEM((192, 800), F32)],
        flops=15_000_000_000,
        size=4 << 20,
        limit=SOME,
    )
    branch_out = jax.ShapeDtypeStruct((192, 400), BF16)
    partial = jax.ShapeDtypeStruct((8, 56, 800), BF16)
    fm_out, lcb_out, keep, send = call(
        rows_kernel,
        (branch_out, branch_out, partial, partial),
        [recv, weights, mix_full, fm_cot[0].T, lcb_cot[0].T],
        [
            pltpu.VMEM((2, 800, 128), F32),
            pltpu.VMEM((2, 128, 800), F32),
            pltpu.VMEM((192, 800), F32),
            pltpu.VMEM((448, 192), F32),
            pltpu.VMEM((448, 192), F32),
        ],
        limit=SOME,
        flops=700_000_000,
        size=5 << 20,
    )

    got = lax.ppermute(send, "rep", SWAP)
    pair = (keep.astype(F32) + got.astype(F32)).astype(BF16)
    shares = lax.all_to_all(pair, TP, 0, 0, tiled=True)
    share = jnp.sum(shares.astype(F32), axis=0).astype(BF16)
    share = jnp.pad(share, ((0, 8), (0, 224)))
    tiles = jnp.transpose(share.reshape(4, 16, 8, 128), (2, 0, 1, 3)).reshape(32, 16, 128)
    parts = lax.all_to_all(tiles, TAB, 0, 0, tiled=True)
    whole = jnp.sum(parts.astype(F32), axis=0).astype(BF16)
    spread = lax.all_to_all(jnp.broadcast_to(whole[None], (32, 16, 128)), TAB, 0, 0, tiled=True)
    swapped = lax.ppermute(spread, "rep", SWAP)

    def rows_of(blocks):
        wide = jnp.transpose(blocks.reshape(8, 4, 16, 128), (1, 2, 0, 3)).reshape(64, 1024)
        return wide[:50, :800].astype(F32)

    grad_a, grad_b = rows_of(spread), rows_of(swapped)
    first = lax.axis_index("rep") == 0
    grad_fm = jnp.where(first, grad_a, grad_b)
    grad_lcb = jnp.where(first, grad_b, grad_a)
    return fm_out.T[None], lcb_out.T[None], grad_fm, grad_lcb


def solution(mesh):
    fine = Mesh(mesh.devices.reshape(2, 8, 4, 2, 4), ("rep", "z", "yh", "yl", "x"))
    samples = ("rep", "yl", "x") + TAB
    in_specs = (
        P(("rep", "yl", "x"), TAB, None),
        P(TAB),
        P(TAB, None, ("rep", "yl", "x")),
        P(TP, None),
        P(TP, None),
        P(TP, None),
        P(samples, None, None),
        P(samples, None, None),
    )
    out_specs = (P(samples, None, None), P(samples, None, None), P(TP, None), P(TP, None))
    return jax.shard_map(per_device, mesh=fine, in_specs=in_specs, out_specs=out_specs, check_vma=False)
```

```python
import functools

import jax
import jax.numpy as jnp
from jax import lax
from jax.experimental import pallas as pl
from jax.experimental.pallas import tpu as pltpu
from jax.sharding import Mesh
from jax.sharding import PartitionSpec as P

F32 = jnp.float32
BF16 = jnp.bfloat16
EPS = 1e-06
SOME = 16 * 1024 * 1024
SWAP = [(0, 1), (1, 0)]
TAB = ("z", "yh")
TP = ("yl", "x")

VM = pl.BlockSpec(memory_space=pltpu.VMEM)
SM = pl.BlockSpec(memory_space=pltpu.SMEM)


def call(kernel, outs, ins, scratch=(), flops=0, size=0, limit=None):
    return pl.pallas_call(
        kernel,
        out_shape=outs,
        in_specs=[VM] * len(ins),
        out_specs=jax.tree.map(lambda _: VM, outs),
        scratch_shapes=list(scratch),
        compiler_params=pltpu.CompilerParams(vmem_limit_bytes=limit),
        cost_estimate=pl.CostEstimate(flops=flops, bytes_accessed=size, transcendentals=0),
    )(*ins)


def nt_dot(a, b):
    return lax.dot_general(a, b, (((1,), (1,)), ((), ())), preferred_element_type=F32)


def nn_dot(a, b):
    return lax.dot_general(a, b, (((1,), (0,)), ((), ())), preferred_element_type=F32)


def mask_kernel(steps_ref, proj_any, own_ref, proj_ref, rows_ref, sem):
    copy = pltpu.make_async_copy(proj_any, proj_ref, sem.at[0])
    copy.start()
    tables, widest = proj_ref.shape[1], proj_ref.shape[2]
    columns = lax.broadcasted_iota(jnp.int32, (tables, widest), 1)
    table = lax.broadcasted_iota(jnp.int32, (tables, 128), 0)
    width = jnp.zeros((tables, 128), jnp.int32)
    for t in range(tables):
        width = jnp.where(table == t, widest // 8 * steps_ref[t], width)
    keep = columns < jnp.concatenate([width] * (widest // 128), axis=1)
    rows_ref[...] = jnp.zeros_like(rows_ref)
    copy.wait()
    for j in range(12):
        masked = jnp.where(keep, proj_ref[j].astype(F32), 0.0)
        for c in range(4):
            rows_ref[c, pl.ds(j, tables, stride=12), :] = masked[:, 128 * c : 128 * c + 128]
    for p in range(own_ref.shape[0]):
        for c in range(4):
            own_ref[p, :, 128 * c : 128 * c + 128] = rows_ref[c, 24 * p : 24 * p + 24, :].astype(BF16)


def pack_kernel(fm_any, lcb_any, mix_any, pack_ref, branch_ref, mix_ref, sems):
    rep = lax.axis_index("rep")
    mix_copy = pltpu.make_async_copy(mix_any, mix_ref, sems.at[1])
    mix_copy.start()
    for k, source in enumerate((fm_any, lcb_any)):
        @pl.when(rep == k)
        def _():
            copy = pltpu.make_async_copy(source, branch_ref, sems.at[0])
            copy.start()
            copy.wait()
    mix_copy.wait()
    pack_ref[...] = jnp.zeros_like(pack_ref)
    rows, cols = branch_ref.shape
    for j in range(7):
        wide = min(128, cols - 128 * j)
        pack_ref[j, :rows, :wide] = branch_ref[:, 128 * j : 128 * j + wide]
    for j in range(2):
        start = pl.multiple_of(rep * 96 + 48 * j, 16)
        pack_ref[7 + j, :48, : mix_ref.shape[1]] = mix_ref[pl.ds(start, 48), :]


def unpack_kernel(small_ref, branch_ref, mix_ref, wide_ref, mixw_ref):
    for k in range(2):
        for i in range(8):
            piece = small_ref.at[8 * k + i]
            for j in range(7):
                wide_ref[50 * i : 50 * i + 50, 128 * j : 128 * j + 128] = piece[j][:50].astype(F32)
            for j in range(2):
                row = 96 * k + 48 * j
                mixw_ref[row : row + 48, 100 * i : 100 * i + 100] = piece[7 + j][:48, :100].astype(F32)
        branch_ref[k] = wide_ref[:, :800].astype(BF16)
    mix_ref[...] = mixw_ref[...].astype(BF16)


def hold_kernel(src_ref, out_ref):
    del src_ref, out_ref


def project_kernel(emb_ref, emb_y_ref, *rest):
    w_refs, out_ref, acc_ref = rest[:-2], rest[-2], rest[-1]
    mine = lax.axis_index("yl")
    far_cut = w_refs[2].shape[0]
    tables, samples = emb_ref.shape[0], emb_ref.shape[1]
    free = lax.broadcasted_iota(jnp.int32, (samples, 128), 1) % 16 >= 12
    last = tables - 1
    extra = {}
    for t in [last] + list(range(last)):
        pair, odd = t // 2, t % 2
        far = w_refs[2].at[pair] if pair < far_cut else w_refs[3].at[pair - far_cut]
        blocks = [w_refs[0].at[pair], w_refs[1].at[pair], far] + [ref.at[pair] for ref in w_refs[4:]]
        weight = jnp.concatenate([block[8 * odd : 8 * odd + 16, :] for block in blocks], axis=0)
        for k, ref in enumerate((emb_ref, emb_y_ref)):
            prod = nt_dot(ref[t], weight)
            if odd:
                prod = pltpu.roll(prod, 124, 1)
            if t == last:
                extra[k] = [pltpu.roll(prod, shift, 1) for shift in (12, 8, 4)]
            else:
                prod = jnp.where(free, extra[k][t] if t < 3 else 0.0, prod)
                slot = mine if k == 0 else 1 - mine
                acc_ref[slot, pl.ds(t, samples, stride=last), :] = prod
    for k in range(2):
        out_ref[k * samples : k * samples + samples] = acc_ref[k].reshape(samples, last, 128).astype(BF16)


def rows_kernel(recv_ref, weight_ref, mix_ref, fcot_ref, lcot_ref,
                fo_ref, lo_ref, keep_ref, send_ref, scr_ref, gt_ref, ft_ref, bf_ref, bl_ref):
    x, rep = lax.axis_index("x"), lax.axis_index("rep")
    place = lax.broadcasted_iota(jnp.int32, (32, 128), 1) % 16
    for yl in range(2):
        for tab in range(32):
            scr_ref[yl, 25 * tab : 25 * tab + 24, :] = recv_ref[yl * 32 + tab].astype(F32)
        last = [pltpu.roll(scr_ref[yl, pl.ds(k, 32, stride=25), :], 116 + 4 * k, 1) for k in range(3)]
        scr_ref[yl, pl.ds(24, 32, stride=25), :] = jnp.where(place < 4, last[0], jnp.where(place < 8, last[1], last[2]))
        gt_ref[yl] = scr_ref[yl].T
    for r in range(2):
        for yl in range(2):
            for spot in range(4):
                far = jnp.bitwise_xor(x, spot)
                start = pl.multiple_of((r + rep - 2 * r * rep) * 64 + far * 16, 16)
                row = r * 96 + yl * 48 + spot * 12
                ft_ref[row : row + 12, :] = gt_ref[yl, pl.ds(start, 16), :][:12]
    feat = ft_ref[...]
    feat_b = feat.astype(BF16)
    inner = nt_dot(mix_ref[...], feat_b)
    high = inner.astype(BF16)
    low = (inner - high.astype(F32)).astype(BF16)
    mixed_b = ((nn_dot(high, feat_b) + nn_dot(low, feat_b)) * (1.0 / 192)).astype(BF16)

    def branch(rows, weight, skip, cot_ref, out_ref, back_ref):
        pre = nt_dot(rows, weight) + skip
        inv = lax.rsqrt(jnp.sum(pre * pre, axis=0, keepdims=True) * (1.0 / 192) + EPS)
        normed = pre * inv
        out_ref[...] = normed.astype(BF16)
        cot = cot_ref[...].astype(F32)
        mean = jnp.sum(cot * normed, axis=0, keepdims=True) * (1.0 / 192)
        back = (inv * (cot - normed * mean)).T
        back_ref[...] = jnp.zeros_like(back_ref)
        for i in range(8):
            back_ref[56 * i : 56 * i + 50, :] = back[50 * i : 50 * i + 50]
        return back_ref[...].astype(BF16)

    back_l = branch(feat_b, weight_ref[1], ft_ref[:, 400:800], lcot_ref, lo_ref, bl_ref)
    back_f = branch(mixed_b, weight_ref[0], ft_ref[:, :400], fcot_ref, fo_ref, bf_ref)
    first = jnp.full((1, 1), rep, jnp.int32) == 0
    keep = nn_dot(jnp.where(first, back_f, back_l), jnp.where(first, mixed_b, feat_b))
    send = nn_dot(jnp.where(first, back_l, back_f), jnp.where(first, feat_b, mixed_b))
    for i in range(8):
        keep_ref[i] = keep[56 * i : 56 * i + 56].astype(BF16)
        send_ref[i] = send[56 * i : 56 * i + 56].astype(BF16)


def per_device(emb_rows, width_steps, proj_weight, fm_weight, lcb_weight, mix_weight, fm_cot, lcb_cot):
    tables, widest = emb_rows.shape[1], emb_rows.shape[2]
    emb = jnp.transpose(emb_rows, (1, 0, 2))
    emb_y = lax.ppermute(emb, "yl", SWAP)
    emb_y = pl.pallas_call(
        hold_kernel,
        out_shape=jax.ShapeDtypeStruct(emb.shape, BF16),
        in_specs=[pl.BlockSpec(memory_space=pl.ANY)],
        out_specs=pl.BlockSpec(memory_space=pl.ANY),
        input_output_aliases={0: 0},
        compiler_params=pltpu.CompilerParams(vmem_limit_bytes=1 << 20),
        cost_estimate=pl.CostEstimate(flops=30_000_000_000, bytes_accessed=0, transcendentals=0),
    )(emb_y)

    pairs = (tables + 1) // 2
    proj = jnp.transpose(proj_weight, (2, 0, 1))
    own = pl.pallas_call(
        mask_kernel,
        out_shape=jax.ShapeDtypeStruct((pairs, 24, widest), BF16),
        in_specs=[SM, pl.BlockSpec(memory_space=pl.ANY)],
        out_specs=VM,
        scratch_shapes=[
            pltpu.VMEM(proj.shape, BF16),
            pltpu.VMEM((4, 24 * pairs, 128), F32),
            pltpu.SemaphoreType.DMA((1,)),
        ],
        cost_estimate=pl.CostEstimate(flops=1 << 20, bytes_accessed=1 << 20, transcendentals=0),
    )(width_steps, proj)
    packed = pl.pallas_call(
        pack_kernel,
        out_shape=jax.ShapeDtypeStruct((9, 56, 128), BF16),
        in_specs=[pl.BlockSpec(memory_space=pl.ANY)] * 3,
        out_specs=VM,
        scratch_shapes=[
            pltpu.VMEM(fm_weight.shape, BF16),
            pltpu.VMEM(mix_weight.shape[::-1], BF16),
            pltpu.SemaphoreType.DMA((2,)),
        ],
        compiler_params=pltpu.CompilerParams(vmem_limit_bytes=2 * 1024 * 1024),
        cost_estimate=pl.CostEstimate(flops=1 << 20, bytes_accessed=1 << 20, transcendentals=0),
    )(fm_weight, lcb_weight, mix_weight.T)
    small = lax.all_gather(packed, ("rep",) + TP)

    side, back = [(i, i ^ 1) for i in range(4)], [(i, i ^ 3) for i in range(4)]
    half = (pairs + 1) // 2
    near = lax.ppermute(own, "x", side)
    next_ = lax.ppermute(own, "x", back)
    own_o = lax.ppermute(own, "rep", SWAP)
    near, own_o = lax.optimization_barrier((near, own_o))
    far_a = lax.ppermute(near[:half], "x", back)
    far_b = lax.ppermute(next_[half:], "x", side)
    near_o = lax.ppermute(near, "rep", SWAP)
    next_o = lax.ppermute(next_, "rep", SWAP)
    far, emb_y = lax.optimization_barrier((jnp.concatenate([far_a, far_b], axis=0), emb_y))
    far_o = lax.ppermute(far, "rep", SWAP)
    mine = [own, near, far_a, far_b, next_]
    other = [own_o, near_o, far_o, next_o]

    chunks = call(
        project_kernel,
        jax.ShapeDtypeStruct((64, 24, 128), BF16),
        [emb, emb_y] + mine + other,
        [pltpu.VMEM((2, 768, 128), F32)],
        limit=SOME,
        flops=2 * 25 * 64 * 128 * 512,
        size=5 << 20,
    )
    recv = lax.all_to_all(chunks, ("yl",) + TAB, 0, 0, tiled=True)

    weights, mix_full = call(
        unpack_kernel,
        (jax.ShapeDtypeStruct((2, 400, 800), BF16), jax.ShapeDtypeStruct((192, 800), BF16)),
        [small],
        [pltpu.VMEM((400, 896), F32), pltpu.VMEM((192, 800), F32)],
        flops=5_000_000_000,
        size=4 << 20,
        limit=SOME,
    )
    branch_out = jax.ShapeDtypeStruct((192, 400), BF16)
    partial = jax.ShapeDtypeStruct((8, 56, 800), BF16)
    fm_out, lcb_out, keep, send = call(
        rows_kernel,
        (branch_out, branch_out, partial, partial),
        [recv, weights, mix_full, fm_cot[0].T, lcb_cot[0].T],
        [
            pltpu.VMEM((2, 800, 128), F32),
            pltpu.VMEM((2, 128, 800), F32),
            pltpu.VMEM((192, 800), F32),
            pltpu.VMEM((448, 192), F32),
            pltpu.VMEM((448, 192), F32),
        ],
        limit=SOME,
        flops=700_000_000,
        size=5 << 20,
    )

    got = lax.ppermute(send, "rep", SWAP)
    pair = (keep.astype(F32) + got.astype(F32)).astype(BF16)
    shares = lax.all_to_all(pair, TP, 0, 0, tiled=True)
    share = jnp.sum(shares.astype(F32), axis=0).astype(BF16)
    share = jnp.pad(share, ((0, 8), (0, 224)))
    tiles = jnp.transpose(share.reshape(4, 16, 8, 128), (2, 0, 1, 3)).reshape(32, 16, 128)
    parts = lax.all_to_all(tiles, TAB, 0, 0, tiled=True)
    whole = jnp.sum(parts.astype(F32), axis=0).astype(BF16)
    spread = lax.all_to_all(jnp.broadcast_to(whole[None], (32, 16, 128)), TAB, 0, 0, tiled=True)
    swapped = lax.ppermute(spread, "rep", SWAP)

    def rows_of(blocks):
        wide = jnp.transpose(blocks.reshape(8, 4, 16, 128), (1, 2, 0, 3)).reshape(64, 1024)
        return wide[:50, :800].astype(F32)

    grad_a, grad_b = rows_of(spread), rows_of(swapped)
    first = lax.axis_index("rep") == 0
    grad_fm = jnp.where(first, grad_a, grad_b)
    grad_lcb = jnp.where(first, grad_b, grad_a)
    return fm_out.T[None], lcb_out.T[None], grad_fm, grad_lcb


def solution(mesh):
    fine = Mesh(mesh.devices.reshape(2, 8, 4, 2, 4), ("rep", "z", "yh", "yl", "x"))
    samples = ("rep", "yl", "x") + TAB
    in_specs = (
        P(("rep", "yl", "x"), TAB, None),
        P(TAB),
        P(TAB, None, ("rep", "yl", "x")),
        P(TP, None),
        P(TP, None),
        P(TP, None),
        P(samples, None, None),
        P(samples, None, None),
    )
    out_specs = (P(samples, None, None), P(samples, None, None), P(TP, None), P(TP, None))
    return jax.shard_map(per_device, mesh=fine, in_specs=in_specs, out_specs=out_specs, check_vma=False)
```

```python
import functools

import jax
import jax.numpy as jnp
from jax import lax
from jax.experimental import pallas as pl
from jax.experimental.pallas import tpu as pltpu
from jax.sharding import Mesh
from jax.sharding import PartitionSpec as P

F32 = jnp.float32
BF16 = jnp.bfloat16
EPS = 1e-06
SOME = 16 * 1024 * 1024
SWAP = [(0, 1), (1, 0)]
TAB = ("z", "yh")
TP = ("yl", "x")

VM = pl.BlockSpec(memory_space=pltpu.VMEM)
SM = pl.BlockSpec(memory_space=pltpu.SMEM)


def call(kernel, outs, ins, scratch=(), flops=0, size=0, limit=None):
    return pl.pallas_call(
        kernel,
        out_shape=outs,
        in_specs=[VM] * len(ins),
        out_specs=jax.tree.map(lambda _: VM, outs),
        scratch_shapes=list(scratch),
        compiler_params=pltpu.CompilerParams(vmem_limit_bytes=limit),
        cost_estimate=pl.CostEstimate(flops=flops, bytes_accessed=size, transcendentals=0),
    )(*ins)


def nt_dot(a, b):
    return lax.dot_general(a, b, (((1,), (1,)), ((), ())), preferred_element_type=F32)


def nn_dot(a, b):
    return lax.dot_general(a, b, (((1,), (0,)), ((), ())), preferred_element_type=F32)


def mask_kernel(steps_ref, proj_any, own_ref, proj_ref, rows_ref, sem):
    copy = pltpu.make_async_copy(proj_any, proj_ref, sem.at[0])
    copy.start()
    tables, widest = proj_ref.shape[1], proj_ref.shape[2]
    columns = lax.broadcasted_iota(jnp.int32, (tables, widest), 1)
    table = lax.broadcasted_iota(jnp.int32, (tables, 128), 0)
    width = jnp.zeros((tables, 128), jnp.int32)
    for t in range(tables):
        width = jnp.where(table == t, widest // 8 * steps_ref[t], width)
    keep = columns < jnp.concatenate([width] * (widest // 128), axis=1)
    rows_ref[...] = jnp.zeros_like(rows_ref)
    copy.wait()
    for j in range(12):
        masked = jnp.where(keep, proj_ref[j].astype(F32), 0.0)
        for c in range(4):
            rows_ref[c, pl.ds(j, tables, stride=12), :] = masked[:, 128 * c : 128 * c + 128]
    for p in range(own_ref.shape[0]):
        for c in range(4):
            own_ref[p, :, 128 * c : 128 * c + 128] = rows_ref[c, 24 * p : 24 * p + 24, :].astype(BF16)


def pack_kernel(fm_any, lcb_any, mix_any, pack_ref, branch_ref, mix_ref, sems):
    rep = lax.axis_index("rep")
    mix_copy = pltpu.make_async_copy(mix_any, mix_ref, sems.at[1])
    mix_copy.start()
    for k, source in enumerate((fm_any, lcb_any)):
        @pl.when(rep == k)
        def _():
            copy = pltpu.make_async_copy(source, branch_ref, sems.at[0])
            copy.start()
            copy.wait()
    mix_copy.wait()
    pack_ref[...] = jnp.zeros_like(pack_ref)
    rows, cols = branch_ref.shape
    for j in range(7):
        wide = min(128, cols - 128 * j)
        pack_ref[j, :rows, :wide] = branch_ref[:, 128 * j : 128 * j + wide]
    for j in range(2):
        start = pl.multiple_of(rep * 96 + 48 * j, 16)
        pack_ref[7 + j, :48, : mix_ref.shape[1]] = mix_ref[pl.ds(start, 48), :]


def unpack_kernel(small_ref, branch_ref, mix_ref, wide_ref, mixw_ref):
    for k in range(2):
        for i in range(8):
            piece = small_ref.at[8 * k + i]
            for j in range(7):
                wide_ref[50 * i : 50 * i + 50, 128 * j : 128 * j + 128] = piece[j][:50].astype(F32)
            for j in range(2):
                row = 96 * k + 48 * j
                mixw_ref[row : row + 48, 100 * i : 100 * i + 100] = piece[7 + j][:48, :100].astype(F32)
        branch_ref[k] = wide_ref[:, :800].astype(BF16)
    mix_ref[...] = mixw_ref[...].astype(BF16)


def project_kernel(emb_ref, emb_y_ref, *rest):
    w_refs, out_ref, acc_ref = rest[:-2], rest[-2], rest[-1]
    mine = lax.axis_index("yl")
    far_cut = w_refs[2].shape[0]
    tables, samples = emb_ref.shape[0], emb_ref.shape[1]
    free = lax.broadcasted_iota(jnp.int32, (samples, 128), 1) % 16 >= 12
    last = tables - 1
    extra = {}
    for t in [last] + list(range(last)):
        pair, odd = t // 2, t % 2
        far = w_refs[2].at[pair] if pair < far_cut else w_refs[3].at[pair - far_cut]
        blocks = [w_refs[0].at[pair], w_refs[1].at[pair], far] + [ref.at[pair] for ref in w_refs[4:]]
        weight = jnp.concatenate([block[8 * odd : 8 * odd + 16, :] for block in blocks], axis=0)
        for k, ref in enumerate((emb_ref, emb_y_ref)):
            prod = nt_dot(ref[t], weight)
            if odd:
                prod = pltpu.roll(prod, 124, 1)
            if t == last:
                extra[k] = [pltpu.roll(prod, shift, 1) for shift in (12, 8, 4)]
            else:
                prod = jnp.where(free, extra[k][t] if t < 3 else 0.0, prod)
                slot = mine if k == 0 else 1 - mine
                acc_ref[slot, pl.ds(t, samples, stride=last), :] = prod
    for k in range(2):
        out_ref[k * samples : k * samples + samples] = acc_ref[k].reshape(samples, last, 128).astype(BF16)


def rows_kernel(recv_ref, weight_ref, mix_ref, fcot_ref, lcot_ref,
                fo_ref, lo_ref, keep_ref, send_ref, scr_ref, gt_ref, ft_ref, bf_ref, bl_ref):
    x, rep = lax.axis_index("x"), lax.axis_index("rep")
    place = lax.broadcasted_iota(jnp.int32, (32, 128), 1) % 16
    for yl in range(2):
        for tab in range(32):
            scr_ref[yl, 25 * tab : 25 * tab + 24, :] = recv_ref[yl * 32 + tab].astype(F32)
        last = [pltpu.roll(scr_ref[yl, pl.ds(k, 32, stride=25), :], 116 + 4 * k, 1) for k in range(3)]
        scr_ref[yl, pl.ds(24, 32, stride=25), :] = jnp.where(place < 4, last[0], jnp.where(place < 8, last[1], last[2]))
        gt_ref[yl] = scr_ref[yl].T
    for r in range(2):
        for yl in range(2):
            for spot in range(4):
                far = jnp.bitwise_xor(x, spot)
                start = pl.multiple_of((r + rep - 2 * r * rep) * 64 + far * 16, 16)
                row = r * 96 + yl * 48 + spot * 12
                ft_ref[row : row + 12, :] = gt_ref[yl, pl.ds(start, 16), :][:12]
    feat = ft_ref[...]
    feat_b = feat.astype(BF16)
    inner = nt_dot(mix_ref[...], feat_b)
    high = inner.astype(BF16)
    low = (inner - high.astype(F32)).astype(BF16)
    mixed_b = ((nn_dot(high, feat_b) + nn_dot(low, feat_b)) * (1.0 / 192)).astype(BF16)

    def branch(rows, weight, skip, cot_ref, out_ref, back_ref):
        pre = nt_dot(rows, weight) + skip
        inv = lax.rsqrt(jnp.sum(pre * pre, axis=0, keepdims=True) * (1.0 / 192) + EPS)
        normed = pre * inv
        out_ref[...] = normed.astype(BF16)
        cot = cot_ref[...].astype(F32)
        mean = jnp.sum(cot * normed, axis=0, keepdims=True) * (1.0 / 192)
        back = (inv * (cot - normed * mean)).T
        back_ref[...] = jnp.zeros_like(back_ref)
        for i in range(8):
            back_ref[56 * i : 56 * i + 50, :] = back[50 * i : 50 * i + 50]
        return back_ref[...].astype(BF16)

    back_l = branch(feat_b, weight_ref[1], ft_ref[:, 400:800], lcot_ref, lo_ref, bl_ref)
    back_f = branch(mixed_b, weight_ref[0], ft_ref[:, :400], fcot_ref, fo_ref, bf_ref)
    first = jnp.full((1, 1), rep, jnp.int32) == 0
    keep = nn_dot(jnp.where(first, back_f, back_l), jnp.where(first, mixed_b, feat_b))
    send = nn_dot(jnp.where(first, back_l, back_f), jnp.where(first, feat_b, mixed_b))
    for i in range(8):
        keep_ref[i] = keep[56 * i : 56 * i + 56].astype(BF16)
        send_ref[i] = send[56 * i : 56 * i + 56].astype(BF16)


def per_device(emb_rows, width_steps, proj_weight, fm_weight, lcb_weight, mix_weight, fm_cot, lcb_cot):
    tables, widest = emb_rows.shape[1], emb_rows.shape[2]
    emb = jnp.transpose(emb_rows, (1, 0, 2))
    emb_y = lax.ppermute(emb, "yl", SWAP)

    pairs = (tables + 1) // 2
    proj = jnp.transpose(proj_weight, (2, 0, 1))
    own = pl.pallas_call(
        mask_kernel,
        out_shape=jax.ShapeDtypeStruct((pairs, 24, widest), BF16),
        in_specs=[SM, pl.BlockSpec(memory_space=pl.ANY)],
        out_specs=VM,
        scratch_shapes=[
            pltpu.VMEM(proj.shape, BF16),
            pltpu.VMEM((4, 24 * pairs, 128), F32),
            pltpu.SemaphoreType.DMA((1,)),
        ],
        cost_estimate=pl.CostEstimate(flops=1 << 20, bytes_accessed=1 << 20, transcendentals=0),
    )(width_steps, proj)
    packed = pl.pallas_call(
        pack_kernel,
        out_shape=jax.ShapeDtypeStruct((9, 56, 128), BF16),
        in_specs=[pl.BlockSpec(memory_space=pl.ANY)] * 3,
        out_specs=VM,
        scratch_shapes=[
            pltpu.VMEM(fm_weight.shape, BF16),
            pltpu.VMEM(mix_weight.shape[::-1], BF16),
            pltpu.SemaphoreType.DMA((2,)),
        ],
        compiler_params=pltpu.CompilerParams(vmem_limit_bytes=2 * 1024 * 1024),
        cost_estimate=pl.CostEstimate(flops=1 << 20, bytes_accessed=1 << 20, transcendentals=0),
    )(fm_weight, lcb_weight, mix_weight.T)
    small = lax.all_gather(packed, ("rep",) + TP)

    side, back = [(i, i ^ 1) for i in range(4)], [(i, i ^ 3) for i in range(4)]
    half = (pairs + 1) // 2
    near = lax.ppermute(own, "x", side)
    next_ = lax.ppermute(own, "x", back)
    own_o = lax.ppermute(own, "rep", SWAP)
    far_a = lax.ppermute(near[:half], "x", back)
    far_b = lax.ppermute(next_[half:], "x", side)
    near_o = lax.ppermute(near, "rep", SWAP)
    next_o = lax.ppermute(next_, "rep", SWAP)
    far = jnp.concatenate([far_a, far_b], axis=0)
    far_o = lax.ppermute(far, "rep", SWAP)
    mine = [own, near, far_a, far_b, next_]
    other = [own_o, near_o, far_o, next_o]

    chunks = call(
        project_kernel,
        jax.ShapeDtypeStruct((64, 24, 128), BF16),
        [emb, emb_y] + mine + other,
        [pltpu.VMEM((2, 768, 128), F32)],
        limit=SOME,
        flops=25_000_000_000,
        size=5 << 20,
    )
    recv = lax.all_to_all(chunks, ("yl",) + TAB, 0, 0, tiled=True)

    weights, mix_full = call(
        unpack_kernel,
        (jax.ShapeDtypeStruct((2, 400, 800), BF16), jax.ShapeDtypeStruct((192, 800), BF16)),
        [small],
        [pltpu.VMEM((400, 896), F32), pltpu.VMEM((192, 800), F32)],
        flops=0,
        size=4 << 20,
        limit=SOME,
    )
    branch_out = jax.ShapeDtypeStruct((192, 400), BF16)
    partial = jax.ShapeDtypeStruct((8, 56, 800), BF16)
    fm_out, lcb_out, keep, send = call(
        rows_kernel,
        (branch_out, branch_out, partial, partial),
        [recv, weights, mix_full, fm_cot[0].T, lcb_cot[0].T],
        [
            pltpu.VMEM((2, 800, 128), F32),
            pltpu.VMEM((2, 128, 800), F32),
            pltpu.VMEM((192, 800), F32),
            pltpu.VMEM((448, 192), F32),
            pltpu.VMEM((448, 192), F32),
        ],
        limit=SOME,
        flops=700_000_000,
        size=5 << 20,
    )

    got = lax.ppermute(send, "rep", SWAP)
    pair = (keep.astype(F32) + got.astype(F32)).astype(BF16)
    shares = lax.all_to_all(pair, TP, 0, 0, tiled=True)
    share = jnp.sum(shares.astype(F32), axis=0).astype(BF16)
    share = jnp.pad(share, ((0, 8), (0, 224)))
    tiles = jnp.transpose(share.reshape(4, 16, 8, 128), (2, 0, 1, 3)).reshape(32, 16, 128)
    parts = lax.all_to_all(tiles, TAB, 0, 0, tiled=True)
    whole = jnp.sum(parts.astype(F32), axis=0).astype(BF16)
    spread = lax.all_to_all(jnp.broadcast_to(whole[None], (32, 16, 128)), TAB, 0, 0, tiled=True)
    swapped = lax.ppermute(spread, "rep", SWAP)

    def rows_of(blocks):
        wide = jnp.transpose(blocks.reshape(8, 4, 16, 128), (1, 2, 0, 3)).reshape(64, 1024)
        return wide[:50, :800].astype(F32)

    grad_a, grad_b = rows_of(spread), rows_of(swapped)
    first = lax.axis_index("rep") == 0
    grad_fm = jnp.where(first, grad_a, grad_b)
    grad_lcb = jnp.where(first, grad_b, grad_a)
    return fm_out.T[None], lcb_out.T[None], grad_fm, grad_lcb


def solution(mesh):
    fine = Mesh(mesh.devices.reshape(2, 8, 4, 2, 4), ("rep", "z", "yh", "yl", "x"))
    samples = ("rep", "yl", "x") + TAB
    in_specs = (
        P(("rep", "yl", "x"), TAB, None),
        P(TAB),
        P(TAB, None, ("rep", "yl", "x")),
        P(TP, None),
        P(TP, None),
        P(TP, None),
        P(samples, None, None),
        P(samples, None, None),
    )
    out_specs = (P(samples, None, None), P(samples, None, None), P(TP, None), P(TP, None))
    return jax.shard_map(per_device, mesh=fine, in_specs=in_specs, out_specs=out_specs, check_vma=False)
```

```python
import functools

import jax
import jax.numpy as jnp
from jax import lax
from jax.experimental import pallas as pl
from jax.experimental.pallas import tpu as pltpu
from jax.sharding import Mesh
from jax.sharding import PartitionSpec as P

F32 = jnp.float32
BF16 = jnp.bfloat16
EPS = 1e-06
SOME = 16 * 1024 * 1024
SWAP = [(0, 1), (1, 0)]
TAB = ("z", "yh")
TP = ("yl", "x")

VM = pl.BlockSpec(memory_space=pltpu.VMEM)
SM = pl.BlockSpec(memory_space=pltpu.SMEM)


def call(kernel, outs, ins, scratch=(), flops=0, size=0, limit=None):
    return pl.pallas_call(
        kernel,
        out_shape=outs,
        in_specs=[VM] * len(ins),
        out_specs=jax.tree.map(lambda _: VM, outs),
        scratch_shapes=list(scratch),
        compiler_params=pltpu.CompilerParams(vmem_limit_bytes=limit),
        cost_estimate=pl.CostEstimate(flops=flops, bytes_accessed=size, transcendentals=0),
    )(*ins)


def nt_dot(a, b):
    return lax.dot_general(a, b, (((1,), (1,)), ((), ())), preferred_element_type=F32)


def nn_dot(a, b):
    return lax.dot_general(a, b, (((1,), (0,)), ((), ())), preferred_element_type=F32)


def prep_kernel(steps_ref, proj_any, fm_any, lcb_any, mix_any, own_ref, pack_ref,
                proj_ref, fm_ref, lcb_ref, mix_ref, rows_ref, sems):
    copies = [
        pltpu.make_async_copy(src, dst, sems.at[k])
        for k, (src, dst) in enumerate(((proj_any, proj_ref), (fm_any, fm_ref), (lcb_any, lcb_ref), (mix_any, mix_ref)))
    ]
    for copy in copies:
        copy.start()
    tables, widest = proj_ref.shape[1], proj_ref.shape[2]
    columns = lax.broadcasted_iota(jnp.int32, (tables, widest), 1)
    table = lax.broadcasted_iota(jnp.int32, (tables, 128), 0)
    width = jnp.zeros((tables, 128), jnp.int32)
    for t in range(tables):
        width = jnp.where(table == t, widest // 8 * steps_ref[t], width)
    keep = columns < jnp.concatenate([width] * (widest // 128), axis=1)
    rows_ref[...] = jnp.zeros_like(rows_ref)
    pack_ref[...] = jnp.zeros_like(pack_ref)
    copies[0].wait()
    for j in range(12):
        masked = jnp.where(keep, proj_ref[j].astype(F32), 0.0)
        for c in range(4):
            rows_ref[c, pl.ds(j, tables, stride=12), :] = masked[:, 128 * c : 128 * c + 128]
    for p in range(own_ref.shape[0]):
        for c in range(4):
            own_ref[p, :, 128 * c : 128 * c + 128] = rows_ref[c, 24 * p : 24 * p + 24, :].astype(BF16)
    for copy in copies[1:]:
        copy.wait()
    rep = lax.axis_index("rep")
    first = jnp.full((1, 1), rep, jnp.int32) == 0
    branch = jnp.where(first, fm_ref[...], lcb_ref[...])
    rows, cols = branch.shape
    for j in range(7):
        wide = min(128, cols - 128 * j)
        pack_ref[j, :rows, :wide] = branch[:, 128 * j : 128 * j + wide]
    for j in range(2):
        start = pl.multiple_of(rep * 96 + 48 * j, 16)
        pack_ref[7 + j, :48, : mix_ref.shape[1]] = mix_ref[pl.ds(start, 48), :]


def unpack_kernel(small_ref, branch_ref, mix_ref, wide_ref, mixw_ref):
    for k in range(2):
        for i in range(8):
            piece = small_ref.at[8 * k + i]
            for j in range(7):
                wide_ref[50 * i : 50 * i + 50, 128 * j : 128 * j + 128] = piece[j][:50].astype(F32)
            for j in range(2):
                row = 96 * k + 48 * j
                mixw_ref[row : row + 48, 100 * i : 100 * i + 100] = piece[7 + j][:48, :100].astype(F32)
        branch_ref[k] = wide_ref[:, :800].astype(BF16)
    mix_ref[...] = mixw_ref[...].astype(BF16)


def project_kernel(emb_ref, emb_y_ref, *rest):
    w_refs, out_ref, acc_ref = rest[:-2], rest[-2], rest[-1]
    mine = lax.axis_index("yl")
    far_cut = w_refs[2].shape[0]
    tables, samples = emb_ref.shape[0], emb_ref.shape[1]
    free = lax.broadcasted_iota(jnp.int32, (samples, 128), 1) % 16 >= 12
    last = tables - 1
    extra = {}
    for t in [last] + list(range(last)):
        pair, odd = t // 2, t % 2
        far = w_refs[2].at[pair] if pair < far_cut else w_refs[3].at[pair - far_cut]
        blocks = [w_refs[0].at[pair], w_refs[1].at[pair], far] + [ref.at[pair] for ref in w_refs[4:]]
        weight = jnp.concatenate([block[8 * odd : 8 * odd + 16, :] for block in blocks], axis=0)
        for k, ref in enumerate((emb_ref, emb_y_ref)):
            prod = nt_dot(ref[t], weight)
            if odd:
                prod = pltpu.roll(prod, 124, 1)
            if t == last:
                extra[k] = [pltpu.roll(prod, shift, 1) for shift in (12, 8, 4)]
            else:
                prod = jnp.where(free, extra[k][t] if t < 3 else 0.0, prod)
                slot = mine if k == 0 else 1 - mine
                acc_ref[slot, pl.ds(t, samples, stride=last), :] = prod
    for k in range(2):
        out_ref[k * samples : k * samples + samples] = acc_ref[k].reshape(samples, last, 128).astype(BF16)


def rows_kernel(recv_ref, weight_ref, mix_ref, fcot_ref, lcot_ref,
                fo_ref, lo_ref, keep_ref, send_ref, scr_ref, gt_ref, ft_ref, bf_ref, bl_ref):
    x, rep = lax.axis_index("x"), lax.axis_index("rep")
    place = lax.broadcasted_iota(jnp.int32, (32, 128), 1) % 16
    for yl in range(2):
        for tab in range(32):
            scr_ref[yl, 25 * tab : 25 * tab + 24, :] = recv_ref[yl * 32 + tab].astype(F32)
        last = [pltpu.roll(scr_ref[yl, pl.ds(k, 32, stride=25), :], 116 + 4 * k, 1) for k in range(3)]
        scr_ref[yl, pl.ds(24, 32, stride=25), :] = jnp.where(place < 4, last[0], jnp.where(place < 8, last[1], last[2]))
        gt_ref[yl] = scr_ref[yl].T
    for r in range(2):
        for yl in range(2):
            for spot in range(4):
                far = jnp.bitwise_xor(x, spot)
                start = pl.multiple_of((r + rep - 2 * r * rep) * 64 + far * 16, 16)
                row = r * 96 + yl * 48 + spot * 12
                ft_ref[row : row + 12, :] = gt_ref[yl, pl.ds(start, 16), :][:12]
    feat = ft_ref[...]
    feat_b = feat.astype(BF16)
    inner = nt_dot(mix_ref[...], feat_b)
    high = inner.astype(BF16)
    low = (inner - high.astype(F32)).astype(BF16)
    mixed_b = ((nn_dot(high, feat_b) + nn_dot(low, feat_b)) * (1.0 / 192)).astype(BF16)

    def branch(rows, weight, skip, cot_ref, out_ref, back_ref):
        pre = nt_dot(rows, weight) + skip
        inv = lax.rsqrt(jnp.sum(pre * pre, axis=0, keepdims=True) * (1.0 / 192) + EPS)
        normed = pre * inv
        out_ref[...] = normed.astype(BF16)
        cot = cot_ref[...].astype(F32)
        mean = jnp.sum(cot * normed, axis=0, keepdims=True) * (1.0 / 192)
        back = (inv * (cot - normed * mean)).T
        back_ref[...] = jnp.zeros_like(back_ref)
        for i in range(8):
            back_ref[56 * i : 56 * i + 50, :] = back[50 * i : 50 * i + 50]
        return back_ref[...].astype(BF16)

    back_l = branch(feat_b, weight_ref[1], ft_ref[:, 400:800], lcot_ref, lo_ref, bl_ref)
    back_f = branch(mixed_b, weight_ref[0], ft_ref[:, :400], fcot_ref, fo_ref, bf_ref)
    first = jnp.full((1, 1), rep, jnp.int32) == 0
    keep = nn_dot(jnp.where(first, back_f, back_l), jnp.where(first, mixed_b, feat_b))
    send = nn_dot(jnp.where(first, back_l, back_f), jnp.where(first, feat_b, mixed_b))
    for i in range(8):
        keep_ref[i] = keep[56 * i : 56 * i + 56].astype(BF16)
        send_ref[i] = send[56 * i : 56 * i + 56].astype(BF16)


def per_device(emb_rows, width_steps, proj_weight, fm_weight, lcb_weight, mix_weight, fm_cot, lcb_cot):
    tables, widest = emb_rows.shape[1], emb_rows.shape[2]
    emb = jnp.transpose(emb_rows, (1, 0, 2))
    emb_y = lax.ppermute(emb, "yl", SWAP)

    pairs = (tables + 1) // 2
    proj = jnp.transpose(proj_weight, (2, 0, 1))
    own, packed = pl.pallas_call(
        prep_kernel,
        out_shape=(
            jax.ShapeDtypeStruct((pairs, 24, widest), BF16),
            jax.ShapeDtypeStruct((9, 56, 128), BF16),
        ),
        in_specs=[SM] + [pl.BlockSpec(memory_space=pl.ANY)] * 4,
        out_specs=(VM, VM),
        scratch_shapes=[
            pltpu.VMEM(proj.shape, BF16),
            pltpu.VMEM(fm_weight.shape, BF16),
            pltpu.VMEM(lcb_weight.shape, BF16),
            pltpu.VMEM(mix_weight.shape[::-1], BF16),
            pltpu.VMEM((4, 24 * pairs, 128), F32),
            pltpu.SemaphoreType.DMA((4,)),
        ],
        cost_estimate=pl.CostEstimate(flops=1 << 20, bytes_accessed=2 << 20, transcendentals=0),
    )(width_steps, proj, fm_weight, lcb_weight, mix_weight.T)
    small = lax.all_gather(packed, ("rep",) + TP)

    side, back = [(i, i ^ 1) for i in range(4)], [(i, i ^ 3) for i in range(4)]
    half = (pairs + 1) // 2
    near = lax.ppermute(own, "x", side)
    next_ = lax.ppermute(own, "x", back)
    own_o = lax.ppermute(own, "rep", SWAP)
    far_a = lax.ppermute(near[:half], "x", back)
    far_b = lax.ppermute(next_[half:], "x", side)
    near_o = lax.ppermute(near, "rep", SWAP)
    next_o = lax.ppermute(next_, "rep", SWAP)
    far = jnp.concatenate([far_a, far_b], axis=0)
    far_o = lax.ppermute(far, "rep", SWAP)
    mine = [own, near, far_a, far_b, next_]
    other = [own_o, near_o, far_o, next_o]

    chunks = call(
        project_kernel,
        jax.ShapeDtypeStruct((64, 24, 128), BF16),
        [emb, emb_y] + mine + other,
        [pltpu.VMEM((2, 768, 128), F32)],
        limit=SOME,
        flops=25_000_000_000,
        size=5 << 20,
    )
    recv = lax.all_to_all(chunks, ("yl",) + TAB, 0, 0, tiled=True)

    weights, mix_full = call(
        unpack_kernel,
        (jax.ShapeDtypeStruct((2, 400, 800), BF16), jax.ShapeDtypeStruct((192, 800), BF16)),
        [small],
        [pltpu.VMEM((400, 896), F32), pltpu.VMEM((192, 800), F32)],
        flops=0,
        size=4 << 20,
        limit=SOME,
    )
    branch_out = jax.ShapeDtypeStruct((192, 400), BF16)
    partial = jax.ShapeDtypeStruct((8, 56, 800), BF16)
    fm_out, lcb_out, keep, send = call(
        rows_kernel,
        (branch_out, branch_out, partial, partial),
        [recv, weights, mix_full, fm_cot[0].T, lcb_cot[0].T],
        [
            pltpu.VMEM((2, 800, 128), F32),
            pltpu.VMEM((2, 128, 800), F32),
            pltpu.VMEM((192, 800), F32),
            pltpu.VMEM((448, 192), F32),
            pltpu.VMEM((448, 192), F32),
        ],
        limit=SOME,
        flops=700_000_000,
        size=5 << 20,
    )

    got = lax.ppermute(send, "rep", SWAP)
    pair = (keep.astype(F32) + got.astype(F32)).astype(BF16)
    shares = lax.all_to_all(pair, TP, 0, 0, tiled=True)
    share = jnp.sum(shares.astype(F32), axis=0).astype(BF16)
    share = jnp.pad(share, ((0, 8), (0, 224)))
    tiles = jnp.transpose(share.reshape(4, 16, 8, 128), (2, 0, 1, 3)).reshape(32, 16, 128)
    parts = lax.all_to_all(tiles, TAB, 0, 0, tiled=True)
    whole = jnp.sum(parts.astype(F32), axis=0).astype(BF16)
    spread = lax.all_to_all(jnp.broadcast_to(whole[None], (64, 16, 128)), ("rep",) + TAB, 0, 0, tiled=True)

    def rows_of(blocks):
        wide = jnp.transpose(blocks.reshape(8, 4, 16, 128), (1, 2, 0, 3)).reshape(64, 1024)
        return wide[:50, :800].astype(F32)

    grad_fm, grad_lcb = rows_of(spread[:32]), rows_of(spread[32:])
    return fm_out.T[None], lcb_out.T[None], grad_fm, grad_lcb


def solution(mesh):
    fine = Mesh(mesh.devices.reshape(2, 8, 4, 2, 4), ("rep", "z", "yh", "yl", "x"))
    samples = ("rep", "yl", "x") + TAB
    in_specs = (
        P(("rep", "yl", "x"), TAB, None),
        P(TAB),
        P(TAB, None, ("rep", "yl", "x")),
        P(TP, None),
        P(TP, None),
        P(TP, None),
        P(samples, None, None),
        P(samples, None, None),
    )
    out_specs = (P(samples, None, None), P(samples, None, None), P(TP, None), P(TP, None))
    return jax.shard_map(per_device, mesh=fine, in_specs=in_specs, out_specs=out_specs, check_vma=False)
```

```python
import functools

import jax
import jax.numpy as jnp
from jax import lax
from jax.experimental import pallas as pl
from jax.experimental.pallas import tpu as pltpu
from jax.sharding import Mesh
from jax.sharding import PartitionSpec as P

F32 = jnp.float32
BF16 = jnp.bfloat16
EPS = 1e-06
SOME = 16 * 1024 * 1024
SWAP = [(0, 1), (1, 0)]
TAB = ("z", "yh")
TP = ("yl", "x")

VM = pl.BlockSpec(memory_space=pltpu.VMEM)
SM = pl.BlockSpec(memory_space=pltpu.SMEM)


def call(kernel, outs, ins, scratch=(), flops=0, size=0, limit=None):
    return pl.pallas_call(
        kernel,
        out_shape=outs,
        in_specs=[VM] * len(ins),
        out_specs=jax.tree.map(lambda _: VM, outs),
        scratch_shapes=list(scratch),
        compiler_params=pltpu.CompilerParams(vmem_limit_bytes=limit),
        cost_estimate=pl.CostEstimate(flops=flops, bytes_accessed=size, transcendentals=0),
    )(*ins)


def nt_dot(a, b):
    return lax.dot_general(a, b, (((1,), (1,)), ((), ())), preferred_element_type=F32)


def nn_dot(a, b):
    return lax.dot_general(a, b, (((1,), (0,)), ((), ())), preferred_element_type=F32)


def prep_kernel(steps_ref, proj_any, fm_any, lcb_any, mix_any, own_ref, pack_ref,
                proj_ref, fm_ref, lcb_ref, mix_ref, rows_ref, sems):
    copies = [
        pltpu.make_async_copy(src, dst, sems.at[k])
        for k, (src, dst) in enumerate(((proj_any, proj_ref), (fm_any, fm_ref), (lcb_any, lcb_ref), (mix_any, mix_ref)))
    ]
    for copy in copies:
        copy.start()
    tables, widest = proj_ref.shape[1], proj_ref.shape[2]
    columns = lax.broadcasted_iota(jnp.int32, (tables, widest), 1)
    table = lax.broadcasted_iota(jnp.int32, (tables, 128), 0)
    width = jnp.zeros((tables, 128), jnp.int32)
    for t in range(tables):
        width = jnp.where(table == t, widest // 8 * steps_ref[t], width)
    keep = columns < jnp.concatenate([width] * (widest // 128), axis=1)
    rows_ref[...] = jnp.zeros_like(rows_ref)
    pack_ref[...] = jnp.zeros_like(pack_ref)
    copies[0].wait()
    for j in range(12):
        masked = jnp.where(keep, proj_ref[j].astype(F32), 0.0)
        for c in range(4):
            rows_ref[c, pl.ds(j, tables, stride=12), :] = masked[:, 128 * c : 128 * c + 128]
    for p in range(own_ref.shape[0]):
        for c in range(4):
            own_ref[p, :, 128 * c : 128 * c + 128] = rows_ref[c, 24 * p : 24 * p + 24, :].astype(BF16)
    for copy in copies[1:]:
        copy.wait()
    rep = lax.axis_index("rep")
    first = jnp.full((1, 1), rep, jnp.int32) == 0
    branch = jnp.where(first, fm_ref[...], lcb_ref[...])
    rows, cols = branch.shape
    for j in range(7):
        wide = min(128, cols - 128 * j)
        pack_ref[j, :rows, :wide] = branch[:, 128 * j : 128 * j + wide]
    for j in range(2):
        start = pl.multiple_of(rep * 96 + 48 * j, 16)
        pack_ref[7 + j, :48, : mix_ref.shape[1]] = mix_ref[pl.ds(start, 48), :]


def unpack_kernel(small_ref, branch_ref, mix_ref, wide_ref, mixw_ref):
    mine = lax.axis_index("yl")
    for k in range(2):
        for i in range(8):
            piece = small_ref.at[4 * k + i % 4, jnp.bitwise_xor(mine, i // 4)]
            for j in range(7):
                wide_ref[50 * i : 50 * i + 50, 128 * j : 128 * j + 128] = piece[j][:50].astype(F32)
            for j in range(2):
                row = 96 * k + 48 * j
                mixw_ref[row : row + 48, 100 * i : 100 * i + 100] = piece[7 + j][:48, :100].astype(F32)
        branch_ref[k] = wide_ref[:, :800].astype(BF16)
    mix_ref[...] = mixw_ref[...].astype(BF16)


def project_kernel(emb_ref, emb_y_ref, *rest):
    w_refs, out_ref, acc_ref = rest[:-2], rest[-2], rest[-1]
    mine = lax.axis_index("yl")
    far_cut = w_refs[2].shape[0]
    tables, samples = emb_ref.shape[0], emb_ref.shape[1]
    free = lax.broadcasted_iota(jnp.int32, (samples, 128), 1) % 16 >= 12
    last = tables - 1
    extra = {}
    for t in [last] + list(range(last)):
        pair, odd = t // 2, t % 2
        far = w_refs[2].at[pair] if pair < far_cut else w_refs[3].at[pair - far_cut]
        blocks = [w_refs[0].at[pair], w_refs[1].at[pair], far] + [ref.at[pair] for ref in w_refs[4:]]
        weight = jnp.concatenate([block[8 * odd : 8 * odd + 16, :] for block in blocks], axis=0)
        for k, ref in enumerate((emb_ref, emb_y_ref)):
            prod = nt_dot(ref[t], weight)
            if odd:
                prod = pltpu.roll(prod, 124, 1)
            if t == last:
                extra[k] = [pltpu.roll(prod, shift, 1) for shift in (12, 8, 4)]
            else:
                prod = jnp.where(free, extra[k][t] if t < 3 else 0.0, prod)
                slot = mine if k == 0 else 1 - mine
                acc_ref[slot, pl.ds(t, samples, stride=last), :] = prod
    for k in range(2):
        out_ref[k * samples : k * samples + samples] = acc_ref[k].reshape(samples, last, 128).astype(BF16)


def rows_kernel(recv_ref, weight_ref, mix_ref, fcot_ref, lcot_ref,
                fo_ref, lo_ref, keep_ref, send_ref, scr_ref, gt_ref, ft_ref, bf_ref, bl_ref):
    x, rep = lax.axis_index("x"), lax.axis_index("rep")
    place = lax.broadcasted_iota(jnp.int32, (32, 128), 1) % 16
    for yl in range(2):
        for tab in range(32):
            scr_ref[yl, 25 * tab : 25 * tab + 24, :] = recv_ref[yl * 32 + tab].astype(F32)
        last = [pltpu.roll(scr_ref[yl, pl.ds(k, 32, stride=25), :], 116 + 4 * k, 1) for k in range(3)]
        scr_ref[yl, pl.ds(24, 32, stride=25), :] = jnp.where(place < 4, last[0], jnp.where(place < 8, last[1], last[2]))
        gt_ref[yl] = scr_ref[yl].T
    for r in range(2):
        for yl in range(2):
            for spot in range(4):
                far = jnp.bitwise_xor(x, spot)
                start = pl.multiple_of((r + rep - 2 * r * rep) * 64 + far * 16, 16)
                row = r * 96 + yl * 48 + spot * 12
                ft_ref[row : row + 12, :] = gt_ref[yl, pl.ds(start, 16), :][:12]
    feat = ft_ref[...]
    feat_b = feat.astype(BF16)
    inner = nt_dot(mix_ref[...], feat_b)
    high = inner.astype(BF16)
    low = (inner - high.astype(F32)).astype(BF16)
    mixed_b = ((nn_dot(high, feat_b) + nn_dot(low, feat_b)) * (1.0 / 192)).astype(BF16)

    def branch(rows, weight, skip, cot_ref, out_ref, back_ref):
        pre = nt_dot(rows, weight) + skip
        inv = lax.rsqrt(jnp.sum(pre * pre, axis=0, keepdims=True) * (1.0 / 192) + EPS)
        normed = pre * inv
        out_ref[...] = normed.astype(BF16)
        cot = cot_ref[...].astype(F32)
        mean = jnp.sum(cot * normed, axis=0, keepdims=True) * (1.0 / 192)
        back = (inv * (cot - normed * mean)).T
        back_ref[...] = jnp.zeros_like(back_ref)
        for i in range(8):
            back_ref[56 * i : 56 * i + 50, :] = back[50 * i : 50 * i + 50]
        return back_ref[...].astype(BF16)

    back_l = branch(feat_b, weight_ref[1], ft_ref[:, 400:800], lcot_ref, lo_ref, bl_ref)
    back_f = branch(mixed_b, weight_ref[0], ft_ref[:, :400], fcot_ref, fo_ref, bf_ref)
    first = jnp.full((1, 1), rep, jnp.int32) == 0
    keep = nn_dot(jnp.where(first, back_f, back_l), jnp.where(first, mixed_b, feat_b))
    send = nn_dot(jnp.where(first, back_l, back_f), jnp.where(first, feat_b, mixed_b))
    for i in range(8):
        keep_ref[i] = keep[56 * i : 56 * i + 56].astype(BF16)
        send_ref[i] = send[56 * i : 56 * i + 56].astype(BF16)


def per_device(emb_rows, width_steps, proj_weight, fm_weight, lcb_weight, mix_weight, fm_cot, lcb_cot):
    tables, widest = emb_rows.shape[1], emb_rows.shape[2]
    emb = jnp.transpose(emb_rows, (1, 0, 2))
    emb_y = lax.ppermute(emb, "yl", SWAP)

    pairs = (tables + 1) // 2
    proj = jnp.transpose(proj_weight, (2, 0, 1))
    own, packed = pl.pallas_call(
        prep_kernel,
        out_shape=(
            jax.ShapeDtypeStruct((pairs, 24, widest), BF16),
            jax.ShapeDtypeStruct((9, 56, 128), BF16),
        ),
        in_specs=[SM] + [pl.BlockSpec(memory_space=pl.ANY)] * 4,
        out_specs=(VM, VM),
        scratch_shapes=[
            pltpu.VMEM(proj.shape, BF16),
            pltpu.VMEM(fm_weight.shape, BF16),
            pltpu.VMEM(lcb_weight.shape, BF16),
            pltpu.VMEM(mix_weight.shape[::-1], BF16),
            pltpu.VMEM((4, 24 * pairs, 128), F32),
            pltpu.SemaphoreType.DMA((4,)),
        ],
        cost_estimate=pl.CostEstimate(flops=1 << 20, bytes_accessed=2 << 20, transcendentals=0),
    )(width_steps, proj, fm_weight, lcb_weight, mix_weight.T)
    pair = jnp.stack([packed, lax.ppermute(packed, "yl", SWAP)])
    small = lax.all_gather(pair, ("rep", "x"))

    side, back = [(i, i ^ 1) for i in range(4)], [(i, i ^ 3) for i in range(4)]
    half = (pairs + 1) // 2
    near = lax.ppermute(own, "x", side)
    next_ = lax.ppermute(own, "x", back)
    own_o = lax.ppermute(own, "rep", SWAP)
    far_a = lax.ppermute(near[:half], "x", back)
    far_b = lax.ppermute(next_[half:], "x", side)
    near_o = lax.ppermute(near, "rep", SWAP)
    next_o = lax.ppermute(next_, "rep", SWAP)
    far = jnp.concatenate([far_a, far_b], axis=0)
    far_o = lax.ppermute(far, "rep", SWAP)
    mine = [own, near, far_a, far_b, next_]
    other = [own_o, near_o, far_o, next_o]

    chunks = call(
        project_kernel,
        jax.ShapeDtypeStruct((64, 24, 128), BF16),
        [emb, emb_y] + mine + other,
        [pltpu.VMEM((2, 768, 128), F32)],
        limit=SOME,
        flops=23_000_000_000,
        size=5 << 20,
    )
    recv = lax.all_to_all(chunks, ("yl",) + TAB, 0, 0, tiled=True)

    weights, mix_full = call(
        unpack_kernel,
        (jax.ShapeDtypeStruct((2, 400, 800), BF16), jax.ShapeDtypeStruct((192, 800), BF16)),
        [small],
        [pltpu.VMEM((400, 896), F32), pltpu.VMEM((192, 800), F32)],
        flops=0,
        size=4 << 20,
        limit=SOME,
    )
    branch_out = jax.ShapeDtypeStruct((192, 400), BF16)
    partial = jax.ShapeDtypeStruct((8, 56, 800), BF16)
    fm_out, lcb_out, keep, send = call(
        rows_kernel,
        (branch_out, branch_out, partial, partial),
        [recv, weights, mix_full, fm_cot[0].T, lcb_cot[0].T],
        [
            pltpu.VMEM((2, 800, 128), F32),
            pltpu.VMEM((2, 128, 800), F32),
            pltpu.VMEM((192, 800), F32),
            pltpu.VMEM((448, 192), F32),
            pltpu.VMEM((448, 192), F32),
        ],
        limit=SOME,
        flops=700_000_000,
        size=5 << 20,
    )

    got = lax.ppermute(send, "rep", SWAP)
    pair = (keep.astype(F32) + got.astype(F32)).astype(BF16)
    shares = lax.all_to_all(pair, TP, 0, 0, tiled=True)
    share = jnp.sum(shares.astype(F32), axis=0).astype(BF16)
    share = jnp.pad(share, ((0, 8), (0, 224)))
    tiles = jnp.transpose(share.reshape(4, 16, 8, 128), (2, 0, 1, 3)).reshape(32, 16, 128)
    parts = lax.all_to_all(tiles, TAB, 0, 0, tiled=True)
    whole = jnp.sum(parts.astype(F32), axis=0).astype(BF16)
    spread = lax.all_to_all(jnp.broadcast_to(whole[None], (64, 16, 128)), ("rep",) + TAB, 0, 0, tiled=True)

    def rows_of(blocks):
        wide = jnp.transpose(blocks.reshape(8, 4, 16, 128), (1, 2, 0, 3)).reshape(64, 1024)
        return wide[:50, :800].astype(F32)

    grad_fm, grad_lcb = rows_of(spread[:32]), rows_of(spread[32:])
    return fm_out.T[None], lcb_out.T[None], grad_fm, grad_lcb


def solution(mesh):
    fine = Mesh(mesh.devices.reshape(2, 8, 4, 2, 4), ("rep", "z", "yh", "yl", "x"))
    samples = ("rep", "yl", "x") + TAB
    in_specs = (
        P(("rep", "yl", "x"), TAB, None),
        P(TAB),
        P(TAB, None, ("rep", "yl", "x")),
        P(TP, None),
        P(TP, None),
        P(TP, None),
        P(samples, None, None),
        P(samples, None, None),
    )
    out_specs = (P(samples, None, None), P(samples, None, None), P(TP, None), P(TP, None))
    return jax.shard_map(per_device, mesh=fine, in_specs=in_specs, out_specs=out_specs, check_vma=False)
```

```python
import functools

import jax
import jax.numpy as jnp
from jax import lax
from jax.experimental import pallas as pl
from jax.experimental.pallas import tpu as pltpu
from jax.sharding import Mesh
from jax.sharding import PartitionSpec as P

F32 = jnp.float32
BF16 = jnp.bfloat16
EPS = 1e-06
SOME = 16 * 1024 * 1024
SWAP = [(0, 1), (1, 0)]
TAB = ("z", "yh")
TP = ("yl", "x")

VM = pl.BlockSpec(memory_space=pltpu.VMEM)
SM = pl.BlockSpec(memory_space=pltpu.SMEM)


def call(kernel, outs, ins, scratch=(), flops=0, size=0, limit=None):
    return pl.pallas_call(
        kernel,
        out_shape=outs,
        in_specs=[VM] * len(ins),
        out_specs=jax.tree.map(lambda _: VM, outs),
        scratch_shapes=list(scratch),
        compiler_params=pltpu.CompilerParams(vmem_limit_bytes=limit),
        cost_estimate=pl.CostEstimate(flops=flops, bytes_accessed=size, transcendentals=0),
    )(*ins)


def nt_dot(a, b):
    return lax.dot_general(a, b, (((1,), (1,)), ((), ())), preferred_element_type=F32)


def nn_dot(a, b):
    return lax.dot_general(a, b, (((1,), (0,)), ((), ())), preferred_element_type=F32)


def prep_kernel(steps_ref, proj_any, fm_any, lcb_any, mix_any, own_ref, pack_ref,
                proj_ref, fm_ref, lcb_ref, mix_ref, rows_ref, sems):
    copies = [
        pltpu.make_async_copy(src, dst, sems.at[k])
        for k, (src, dst) in enumerate(((proj_any, proj_ref), (fm_any, fm_ref), (lcb_any, lcb_ref), (mix_any, mix_ref)))
    ]
    for copy in copies:
        copy.start()
    tables, widest = proj_ref.shape[1], proj_ref.shape[2]
    columns = lax.broadcasted_iota(jnp.int32, (tables, widest), 1)
    table = lax.broadcasted_iota(jnp.int32, (tables, 128), 0)
    width = jnp.zeros((tables, 128), jnp.int32)
    for t in range(tables):
        width = jnp.where(table == t, widest // 8 * steps_ref[t], width)
    keep = columns < jnp.concatenate([width] * (widest // 128), axis=1)
    rows_ref[...] = jnp.zeros_like(rows_ref)
    pack_ref[...] = jnp.zeros_like(pack_ref)
    copies[0].wait()
    for j in range(12):
        masked = jnp.where(keep, proj_ref[j].astype(F32), 0.0)
        for c in range(4):
            rows_ref[c, pl.ds(j, tables, stride=12), :] = masked[:, 128 * c : 128 * c + 128]
    for p in range(own_ref.shape[0]):
        for c in range(4):
            own_ref[p, :, 128 * c : 128 * c + 128] = rows_ref[c, 24 * p : 24 * p + 24, :].astype(BF16)
    for copy in copies[1:]:
        copy.wait()
    rep = lax.axis_index("rep")
    first = jnp.full((1, 1), rep, jnp.int32) == 0
    branch = jnp.where(first, fm_ref[...], lcb_ref[...])
    rows, cols = branch.shape
    for j in range(7):
        wide = min(128, cols - 128 * j)
        pack_ref[j, :rows, :wide] = branch[:, 128 * j : 128 * j + wide]
    for j in range(2):
        start = pl.multiple_of(rep * 96 + 48 * j, 16)
        pack_ref[7 + j, :48, : mix_ref.shape[1]] = mix_ref[pl.ds(start, 48), :]


def unpack_kernel(small_ref, branch_ref, mix_ref, wide_ref, mixw_ref):
    mine = lax.axis_index("yl")
    for k in range(2):
        for i in range(8):
            piece = small_ref.at[4 * k + i % 4, jnp.bitwise_xor(mine, i // 4)]
            for j in range(7):
                wide_ref[50 * i : 50 * i + 50, 128 * j : 128 * j + 128] = piece[j][:50].astype(F32)
            for j in range(2):
                row = 96 * k + 48 * j
                mixw_ref[row : row + 48, 100 * i : 100 * i + 100] = piece[7 + j][:48, :100].astype(F32)
        branch_ref[k] = wide_ref[:, :800].astype(BF16)
    mix_ref[...] = mixw_ref[...].astype(BF16)


def project_kernel(emb_ref, emb_y_ref, *rest):
    w_refs, out_ref, acc_ref = rest[:-2], rest[-2], rest[-1]
    mine = lax.axis_index("yl")
    far_cut = w_refs[2].shape[0]
    tables, samples = emb_ref.shape[0], emb_ref.shape[1]
    free = lax.broadcasted_iota(jnp.int32, (samples, 128), 1) % 16 >= 12
    last = tables - 1
    extra = {}
    for t in [last] + list(range(last)):
        pair, odd = t // 2, t % 2
        far = w_refs[2].at[pair] if pair < far_cut else w_refs[3].at[pair - far_cut]
        blocks = [w_refs[0].at[pair], w_refs[1].at[pair], far] + [ref.at[pair] for ref in w_refs[4:]]
        weight = jnp.concatenate([block[8 * odd : 8 * odd + 16, :] for block in blocks], axis=0)
        for k, ref in enumerate((emb_ref, emb_y_ref)):
            prod = nt_dot(ref[t], weight)
            if odd:
                prod = pltpu.roll(prod, 124, 1)
            if t == last:
                extra[k] = [pltpu.roll(prod, shift, 1) for shift in (12, 8, 4)]
            else:
                prod = jnp.where(free, extra[k][t] if t < 3 else 0.0, prod)
                slot = mine if k == 0 else 1 - mine
                acc_ref[slot, pl.ds(t, samples, stride=last), :] = prod
    for k in range(2):
        out_ref[k * samples : k * samples + samples] = acc_ref[k].reshape(samples, last, 128).astype(BF16)


def rows_kernel(recv_ref, weight_ref, mix_ref, fcot_ref, lcot_ref,
                fo_ref, lo_ref, keep_ref, send_ref, scr_ref, gt_ref, ft_ref, bf_ref, bl_ref):
    x, rep = lax.axis_index("x"), lax.axis_index("rep")
    place = lax.broadcasted_iota(jnp.int32, (32, 128), 1) % 16
    for yl in range(2):
        for tab in range(32):
            scr_ref[yl, 25 * tab : 25 * tab + 24, :] = recv_ref[yl * 32 + tab].astype(F32)
        last = [pltpu.roll(scr_ref[yl, pl.ds(k, 32, stride=25), :], 116 + 4 * k, 1) for k in range(3)]
        scr_ref[yl, pl.ds(24, 32, stride=25), :] = jnp.where(place < 4, last[0], jnp.where(place < 8, last[1], last[2]))
        gt_ref[yl] = scr_ref[yl].T
    for r in range(2):
        for yl in range(2):
            for spot in range(4):
                far = jnp.bitwise_xor(x, spot)
                start = pl.multiple_of((r + rep - 2 * r * rep) * 64 + far * 16, 16)
                row = r * 96 + yl * 48 + spot * 12
                ft_ref[row : row + 12, :] = gt_ref[yl, pl.ds(start, 16), :][:12]
    feat = ft_ref[...]
    feat_b = feat.astype(BF16)
    inner = nt_dot(mix_ref[...], feat_b)
    high = inner.astype(BF16)
    low = (inner - high.astype(F32)).astype(BF16)
    mixed_b = ((nn_dot(high, feat_b) + nn_dot(low, feat_b)) * (1.0 / 192)).astype(BF16)

    def branch(rows, weight, skip, cot_ref, out_ref, back_ref):
        pre = nt_dot(rows, weight) + skip
        inv = lax.rsqrt(jnp.sum(pre * pre, axis=0, keepdims=True) * (1.0 / 192) + EPS)
        normed = pre * inv
        out_ref[...] = normed.astype(BF16)
        cot = cot_ref[...].astype(F32)
        mean = jnp.sum(cot * normed, axis=0, keepdims=True) * (1.0 / 192)
        back = (inv * (cot - normed * mean)).T
        back_ref[...] = jnp.zeros_like(back_ref)
        for i in range(8):
            back_ref[56 * i : 56 * i + 50, :] = back[50 * i : 50 * i + 50]
        return back_ref[...].astype(BF16)

    back_l = branch(feat_b, weight_ref[1], ft_ref[:, 400:800], lcot_ref, lo_ref, bl_ref)
    back_f = branch(mixed_b, weight_ref[0], ft_ref[:, :400], fcot_ref, fo_ref, bf_ref)
    first = jnp.full((1, 1), rep, jnp.int32) == 0
    keep = nn_dot(jnp.where(first, back_f, back_l), jnp.where(first, mixed_b, feat_b))
    send = nn_dot(jnp.where(first, back_l, back_f), jnp.where(first, feat_b, mixed_b))
    for i in range(8):
        keep_ref[i] = keep[56 * i : 56 * i + 56].astype(BF16)
        send_ref[i] = send[56 * i : 56 * i + 56].astype(BF16)


def per_device(emb_rows, width_steps, proj_weight, fm_weight, lcb_weight, mix_weight, fm_cot, lcb_cot):
    tables, widest = emb_rows.shape[1], emb_rows.shape[2]
    emb = jnp.transpose(emb_rows, (1, 0, 2))
    emb_y = lax.ppermute(emb, "yl", SWAP)

    pairs = (tables + 1) // 2
    proj = jnp.transpose(proj_weight, (2, 0, 1))
    own, packed = pl.pallas_call(
        prep_kernel,
        out_shape=(
            jax.ShapeDtypeStruct((pairs, 24, widest), BF16),
            jax.ShapeDtypeStruct((9, 56, 128), BF16),
        ),
        in_specs=[SM] + [pl.BlockSpec(memory_space=pl.ANY)] * 4,
        out_specs=(VM, VM),
        scratch_shapes=[
            pltpu.VMEM(proj.shape, BF16),
            pltpu.VMEM(fm_weight.shape, BF16),
            pltpu.VMEM(lcb_weight.shape, BF16),
            pltpu.VMEM(mix_weight.shape[::-1], BF16),
            pltpu.VMEM((4, 24 * pairs, 128), F32),
            pltpu.SemaphoreType.DMA((4,)),
        ],
        cost_estimate=pl.CostEstimate(flops=1 << 20, bytes_accessed=2 << 20, transcendentals=0),
    )(width_steps, proj, fm_weight, lcb_weight, mix_weight.T)
    pair = jnp.stack([packed, lax.ppermute(packed, "yl", SWAP)])
    small = lax.all_gather(pair, ("rep", "x"))

    side, back = [(i, i ^ 1) for i in range(4)], [(i, i ^ 3) for i in range(4)]
    half = (pairs + 1) // 2
    near = lax.ppermute(own, "x", side)
    next_ = lax.ppermute(own, "x", back)
    own_o = lax.ppermute(own, "rep", SWAP)
    far_a = lax.ppermute(near[:half], "x", back)
    far_b = lax.ppermute(next_[half:], "x", side)
    near_o = lax.ppermute(near, "rep", SWAP)
    next_o = lax.ppermute(next_, "rep", SWAP)
    far = jnp.concatenate([far_a, far_b], axis=0)
    far_o = lax.ppermute(far, "rep", SWAP)
    mine = [own, near, far_a, far_b, next_]
    other = [own_o, near_o, far_o, next_o]

    chunks = call(
        project_kernel,
        jax.ShapeDtypeStruct((64, 24, 128), BF16),
        [emb, emb_y] + mine + other,
        [pltpu.VMEM((2, 768, 128), F32)],
        limit=SOME,
        flops=24_000_000_000,
        size=5 << 20,
    )
    recv = lax.all_to_all(chunks, ("yl",) + TAB, 0, 0, tiled=True)

    weights, mix_full = call(
        unpack_kernel,
        (jax.ShapeDtypeStruct((2, 400, 800), BF16), jax.ShapeDtypeStruct((192, 800), BF16)),
        [small],
        [pltpu.VMEM((400, 896), F32), pltpu.VMEM((192, 800), F32)],
        flops=0,
        size=4 << 20,
        limit=SOME,
    )
    branch_out = jax.ShapeDtypeStruct((192, 400), BF16)
    partial = jax.ShapeDtypeStruct((8, 56, 800), BF16)
    fm_out, lcb_out, keep, send = call(
        rows_kernel,
        (branch_out, branch_out, partial, partial),
        [recv, weights, mix_full, fm_cot[0].T, lcb_cot[0].T],
        [
            pltpu.VMEM((2, 800, 128), F32),
            pltpu.VMEM((2, 128, 800), F32),
            pltpu.VMEM((192, 800), F32),
            pltpu.VMEM((448, 192), F32),
            pltpu.VMEM((448, 192), F32),
        ],
        limit=SOME,
        flops=700_000_000,
        size=5 << 20,
    )

    got = lax.ppermute(send, "rep", SWAP)
    pair = (keep.astype(F32) + got.astype(F32)).astype(BF16)
    shares = lax.all_to_all(pair, TP, 0, 0, tiled=True)
    share = jnp.sum(shares.astype(F32), axis=0).astype(BF16)
    share = jnp.pad(share, ((0, 8), (0, 224)))
    tiles = jnp.transpose(share.reshape(4, 16, 8, 128), (2, 0, 1, 3)).reshape(32, 16, 128)
    parts = lax.all_to_all(tiles, TAB, 0, 0, tiled=True)
    whole = jnp.sum(parts.astype(F32), axis=0).astype(BF16)
    spread = lax.all_to_all(jnp.broadcast_to(whole[None], (64, 16, 128)), ("rep",) + TAB, 0, 0, tiled=True)

    def rows_of(blocks):
        wide = jnp.transpose(blocks.reshape(8, 4, 16, 128), (1, 2, 0, 3)).reshape(64, 1024)
        return wide[:50, :800].astype(F32)

    grad_fm, grad_lcb = rows_of(spread[:32]), rows_of(spread[32:])
    return fm_out.T[None], lcb_out.T[None], grad_fm, grad_lcb


def solution(mesh):
    fine = Mesh(mesh.devices.reshape(2, 8, 4, 2, 4), ("rep", "z", "yh", "yl", "x"))
    samples = ("rep", "yl", "x") + TAB
    in_specs = (
        P(("rep", "yl", "x"), TAB, None),
        P(TAB),
        P(TAB, None, ("rep", "yl", "x")),
        P(TP, None),
        P(TP, None),
        P(TP, None),
        P(samples, None, None),
        P(samples, None, None),
    )
    out_specs = (P(samples, None, None), P(samples, None, None), P(TP, None), P(TP, None))
    return jax.shard_map(per_device, mesh=fine, in_specs=in_specs, out_specs=out_specs, check_vma=False)
```

```python
import functools

import jax
import jax.numpy as jnp
from jax import lax
from jax.experimental import pallas as pl
from jax.experimental.pallas import tpu as pltpu
from jax.sharding import Mesh
from jax.sharding import PartitionSpec as P

F32 = jnp.float32
BF16 = jnp.bfloat16
EPS = 1e-06
SOME = 16 * 1024 * 1024
SWAP = [(0, 1), (1, 0)]
TAB = ("z", "yh")
TP = ("yl", "x")

VM = pl.BlockSpec(memory_space=pltpu.VMEM)
SM = pl.BlockSpec(memory_space=pltpu.SMEM)


def call(kernel, outs, ins, scratch=(), flops=0, size=0, limit=None):
    return pl.pallas_call(
        kernel,
        out_shape=outs,
        in_specs=[VM] * len(ins),
        out_specs=jax.tree.map(lambda _: VM, outs),
        scratch_shapes=list(scratch),
        compiler_params=pltpu.CompilerParams(vmem_limit_bytes=limit),
        cost_estimate=pl.CostEstimate(flops=flops, bytes_accessed=size, transcendentals=0),
    )(*ins)


def nt_dot(a, b):
    return lax.dot_general(a, b, (((1,), (1,)), ((), ())), preferred_element_type=F32)


def nn_dot(a, b):
    return lax.dot_general(a, b, (((1,), (0,)), ((), ())), preferred_element_type=F32)


def prep_kernel(steps_ref, proj_any, fm_any, lcb_any, mix_any, own_ref, pack_ref,
                proj_ref, fm_ref, lcb_ref, mix_ref, rows_ref, sems):
    copies = [
        pltpu.make_async_copy(src, dst, sems.at[k])
        for k, (src, dst) in enumerate(((proj_any, proj_ref), (fm_any, fm_ref), (lcb_any, lcb_ref), (mix_any, mix_ref)))
    ]
    for copy in copies:
        copy.start()
    tables, widest = proj_ref.shape[1], proj_ref.shape[2]
    columns = lax.broadcasted_iota(jnp.int32, (tables, widest), 1)
    table = lax.broadcasted_iota(jnp.int32, (tables, 128), 0)
    width = jnp.zeros((tables, 128), jnp.int32)
    for t in range(tables):
        width = jnp.where(table == t, widest // 8 * steps_ref[t], width)
    keep = columns < jnp.concatenate([width] * (widest // 128), axis=1)
    rows_ref[:, 296:312, :] = jnp.zeros((4, 16, 128), F32)
    pack_ref[...] = jnp.zeros_like(pack_ref)
    copies[0].wait()
    for j in range(12):
        masked = jnp.where(keep, proj_ref[j].astype(F32), 0.0)
        for c in range(4):
            rows_ref[c, pl.ds(j, tables, stride=12), :] = masked[:, 128 * c : 128 * c + 128]
    for p in range(own_ref.shape[0]):
        for c in range(4):
            own_ref[p, :, 128 * c : 128 * c + 128] = rows_ref[c, 24 * p : 24 * p + 24, :].astype(BF16)
    for copy in copies[1:]:
        copy.wait()
    rep = lax.axis_index("rep")
    first = jnp.full((1, 1), rep, jnp.int32) == 0
    branch = jnp.where(first, fm_ref[...], lcb_ref[...])
    rows, cols = branch.shape
    for j in range(7):
        wide = min(128, cols - 128 * j)
        pack_ref[j, :rows, :wide] = branch[:, 128 * j : 128 * j + wide]
    for j in range(2):
        start = pl.multiple_of(rep * 96 + 48 * j, 16)
        pack_ref[7 + j, :48, : mix_ref.shape[1]] = mix_ref[pl.ds(start, 48), :]


def unpack_kernel(small_ref, branch_ref, mix_ref, wide_ref, mixw_ref):
    for k in range(2):
        for i in range(8):
            piece = small_ref.at[8 * k + i]
            for j in range(7):
                wide_ref[50 * i : 50 * i + 50, 128 * j : 128 * j + 128] = piece[j][:50].astype(F32)
            for j in range(2):
                row = 96 * k + 48 * j
                mixw_ref[row : row + 48, 100 * i : 100 * i + 100] = piece[7 + j][:48, :100].astype(F32)
        branch_ref[k] = wide_ref[:, :800].astype(BF16)
    mix_ref[...] = mixw_ref[...].astype(BF16)


def project_kernel(emb_ref, emb_y_ref, *rest):
    w_refs, out_ref, acc_ref = rest[:-2], rest[-2], rest[-1]
    mine = lax.axis_index("yl")
    far_cut = w_refs[2].shape[0]
    tables, samples = emb_ref.shape[0], emb_ref.shape[1]
    free = lax.broadcasted_iota(jnp.int32, (samples, 128), 1) % 16 >= 12
    last = tables - 1
    extra = {}
    for t in [last] + list(range(last)):
        pair, odd = t // 2, t % 2
        far = w_refs[2].at[pair] if pair < far_cut else w_refs[3].at[pair - far_cut]
        blocks = [w_refs[0].at[pair], w_refs[1].at[pair], far] + [ref.at[pair] for ref in w_refs[4:]]
        weight = jnp.concatenate([block[8 * odd : 8 * odd + 16, :] for block in blocks], axis=0)
        for k, ref in enumerate((emb_ref, emb_y_ref)):
            prod = nt_dot(ref[t], weight)
            if odd:
                prod = pltpu.roll(prod, 124, 1)
            if t == last:
                extra[k] = [pltpu.roll(prod, shift, 1) for shift in (12, 8, 4)]
            else:
                prod = jnp.where(free, extra[k][t] if t < 3 else 0.0, prod)
                slot = mine if k == 0 else 1 - mine
                acc_ref[slot, pl.ds(t, samples, stride=last), :] = prod
    for k in range(2):
        out_ref[k * samples : k * samples + samples] = acc_ref[k, : samples * last, :].reshape(samples, last, 128).astype(BF16)


def rows_kernel(recv_ref, weight_ref, mix_ref, fcot_ref, lcot_ref,
                fo_ref, lo_ref, keep_ref, send_ref, scr_ref, gt_ref, ft_ref, bf_ref, bl_ref):
    x, rep = lax.axis_index("x"), lax.axis_index("rep")
    place = lax.broadcasted_iota(jnp.int32, (32, 128), 1) % 16
    for yl in range(2):
        for tab in range(32):
            scr_ref[yl, 25 * tab : 25 * tab + 24, :] = recv_ref[yl * 32 + tab].astype(F32)
        last = [pltpu.roll(scr_ref[yl, pl.ds(k, 32, stride=25), :], 116 + 4 * k, 1) for k in range(3)]
        scr_ref[yl, pl.ds(24, 32, stride=25), :] = jnp.where(place < 4, last[0], jnp.where(place < 8, last[1], last[2]))
        gt_ref[yl] = scr_ref[yl, :800, :].T
    for r in range(2):
        for yl in range(2):
            for spot in range(4):
                far = jnp.bitwise_xor(x, spot)
                start = pl.multiple_of((r + rep - 2 * r * rep) * 64 + far * 16, 16)
                row = r * 96 + yl * 48 + spot * 12
                ft_ref[row : row + 12, :] = gt_ref[yl, pl.ds(start, 16), :][:12]
    feat = ft_ref[...]
    feat_b = feat.astype(BF16)
    inner = nt_dot(mix_ref[...], feat_b)
    high = inner.astype(BF16)
    low = (inner - high.astype(F32)).astype(BF16)
    mixed_b = ((nn_dot(high, feat_b) + nn_dot(low, feat_b)) * (1.0 / 192)).astype(BF16)

    def branch(rows, weight, skip, cot_ref, out_ref, back_ref):
        pre = nt_dot(rows, weight) + skip
        inv = lax.rsqrt(jnp.sum(pre * pre, axis=0, keepdims=True) * (1.0 / 192) + EPS)
        normed = pre * inv
        out_ref[...] = normed.astype(BF16)
        cot = cot_ref[...].astype(F32)
        mean = jnp.sum(cot * normed, axis=0, keepdims=True) * (1.0 / 192)
        back = (inv * (cot - normed * mean)).T
        back_ref[...] = jnp.zeros_like(back_ref)
        for i in range(8):
            back_ref[56 * i : 56 * i + 50, :] = back[50 * i : 50 * i + 50]
        return back_ref[...].astype(BF16)

    back_l = branch(feat_b, weight_ref[1], ft_ref[:, 400:800], lcot_ref, lo_ref, bl_ref)
    back_f = branch(mixed_b, weight_ref[0], ft_ref[:, :400], fcot_ref, fo_ref, bf_ref)
    first = jnp.full((1, 1), rep, jnp.int32) == 0
    keep = nn_dot(jnp.where(first, back_f, back_l), jnp.where(first, mixed_b, feat_b))
    send = nn_dot(jnp.where(first, back_l, back_f), jnp.where(first, feat_b, mixed_b))
    for i in range(8):
        keep_ref[i] = keep[56 * i : 56 * i + 56].astype(BF16)
        send_ref[i] = send[56 * i : 56 * i + 56].astype(BF16)


def per_device(emb_rows, width_steps, proj_weight, fm_weight, lcb_weight, mix_weight, fm_cot, lcb_cot):
    tables, widest = emb_rows.shape[1], emb_rows.shape[2]
    emb = jnp.transpose(emb_rows, (1, 0, 2))
    emb_y = lax.ppermute(emb, "yl", SWAP)

    pairs = (tables + 1) // 2
    proj = jnp.transpose(proj_weight, (2, 0, 1))
    own, packed = pl.pallas_call(
        prep_kernel,
        out_shape=(
            jax.ShapeDtypeStruct((pairs, 24, widest), BF16),
            jax.ShapeDtypeStruct((9, 56, 128), BF16),
        ),
        in_specs=[SM] + [pl.BlockSpec(memory_space=pl.ANY)] * 4,
        out_specs=(VM, VM),
        scratch_shapes=[
            pltpu.VMEM(proj.shape, BF16),
            pltpu.VMEM(fm_weight.shape, BF16),
            pltpu.VMEM(lcb_weight.shape, BF16),
            pltpu.VMEM(mix_weight.shape[::-1], BF16),
            pltpu.VMEM((4, 400, 128), F32),
            pltpu.SemaphoreType.DMA((4,)),
        ],
        cost_estimate=pl.CostEstimate(flops=1 << 20, bytes_accessed=2 << 20, transcendentals=0),
    )(width_steps, proj, fm_weight, lcb_weight, mix_weight.T)
    small = lax.all_gather(packed, ("rep",) + TP)

    side, back = [(i, i ^ 1) for i in range(4)], [(i, i ^ 3) for i in range(4)]
    half = (pairs + 1) // 2
    near = lax.ppermute(own, "x", side)
    next_ = lax.ppermute(own, "x", back)
    own_o = lax.ppermute(own, "rep", SWAP)
    far_a = lax.ppermute(near[:half], "x", back)
    far_b = lax.ppermute(next_[half:], "x", side)
    near_o = lax.ppermute(near, "rep", SWAP)
    next_o = lax.ppermute(next_, "rep", SWAP)
    far = jnp.concatenate([far_a, far_b], axis=0)
    far_o = lax.ppermute(far, "rep", SWAP)
    mine = [own, near, far_a, far_b, next_]
    other = [own_o, near_o, far_o, next_o]

    chunks = call(
        project_kernel,
        jax.ShapeDtypeStruct((64, 24, 128), BF16),
        [emb, emb_y] + mine + other,
        [pltpu.VMEM((2, 800, 128), F32)],
        limit=SOME,
        flops=25_000_000_000,
        size=5 << 20,
    )
    recv = lax.all_to_all(chunks, ("yl",) + TAB, 0, 0, tiled=True)

    weights, mix_full = call(
        unpack_kernel,
        (jax.ShapeDtypeStruct((2, 400, 800), BF16), jax.ShapeDtypeStruct((192, 800), BF16)),
        [small],
        [pltpu.VMEM((400, 896), F32), pltpu.VMEM((192, 800), F32)],
        flops=0,
        size=4 << 20,
        limit=SOME,
    )
    branch_out = jax.ShapeDtypeStruct((192, 400), BF16)
    partial = jax.ShapeDtypeStruct((8, 56, 800), BF16)
    fm_out, lcb_out, keep, send = call(
        rows_kernel,
        (branch_out, branch_out, partial, partial),
        [recv, weights, mix_full, fm_cot[0].T, lcb_cot[0].T],
        [
            pltpu.VMEM((2, 832, 128), F32),
            pltpu.VMEM((2, 128, 800), F32),
            pltpu.VMEM((192, 800), F32),
            pltpu.VMEM((448, 192), F32),
            pltpu.VMEM((448, 192), F32),
        ],
        limit=SOME,
        flops=700_000_000,
        size=5 << 20,
    )

    got = lax.ppermute(send, "rep", SWAP)
    pair = (keep.astype(F32) + got.astype(F32)).astype(BF16)
    shares = lax.all_to_all(pair, TP, 0, 0, tiled=True)
    share = jnp.sum(shares.astype(F32), axis=0).astype(BF16)
    share = jnp.pad(share, ((0, 8), (0, 224)))
    tiles = jnp.transpose(share.reshape(4, 16, 8, 128), (2, 0, 1, 3)).reshape(32, 16, 128)
    parts = lax.all_to_all(tiles, TAB, 0, 0, tiled=True)
    whole = jnp.sum(parts.astype(F32), axis=0).astype(BF16)
    spread = lax.all_to_all(jnp.broadcast_to(whole[None], (64, 16, 128)), ("rep",) + TAB, 0, 0, tiled=True)

    def rows_of(blocks):
        wide = jnp.transpose(blocks.reshape(8, 4, 16, 128), (1, 2, 0, 3)).reshape(64, 1024)
        return wide[:50, :800].astype(F32)

    grad_fm, grad_lcb = rows_of(spread[:32]), rows_of(spread[32:])
    return fm_out.T[None], lcb_out.T[None], grad_fm, grad_lcb


def solution(mesh):
    fine = Mesh(mesh.devices.reshape(2, 8, 4, 2, 4), ("rep", "z", "yh", "yl", "x"))
    samples = ("rep", "yl", "x") + TAB
    in_specs = (
        P(("rep", "yl", "x"), TAB, None),
        P(TAB),
        P(TAB, None, ("rep", "yl", "x")),
        P(TP, None),
        P(TP, None),
        P(TP, None),
        P(samples, None, None),
        P(samples, None, None),
    )
    out_specs = (P(samples, None, None), P(samples, None, None), P(TP, None), P(TP, None))
    return jax.shard_map(per_device, mesh=fine, in_specs=in_specs, out_specs=out_specs, check_vma=False)
```
